256 devices in a mesh: dp: 4 (over y), space: 64 (over x, z, core).
Axes of the slice: x: 4, y: 4, z: 8, core: 2. Of those that a mesh axis runs over, the one named last changes fastest.
Arguments:
- features: bfloat16 [65536, 256], P(('dp', 'space')), parts along dimension 0, may hold values from -16 to 16
- conv_weight: bfloat16 [27, 256, 256], replicated, may hold values from -0.125 to 0.125
- down_weight: bfloat16 [8, 256, 256], replicated, may hold values from -0.25 to 0.25
- grad_conv: bfloat16 [65536, 256], P(('dp', 'space')), parts along dimension 0, may hold values from -6 to 6
- grad_down: bfloat16 [32768, 256], P(('dp', 'space')), parts along dimension 0, may hold values from -6 to 6
- live_rows: int32 [256], P(('dp', 'space')), parts along dimension 0, may hold values from 128 to 256, as said below
- halo_send: int32 [256, 128], P(('dp', 'space')), parts along dimension 0, may hold values from -1 to 255, as said below
- neighbors: int32 [27, 65536], P(None, ('dp', 'space')), parts along dimension 1, may hold values from -1 to 383, as said below
- coarse_code: int32 [65536], P(('dp', 'space')), parts along dimension 0, may hold values from -1 to 1023, as said below
Outputs:
- conv_out: bfloat16 [65536, 256], P(('dp', 'space')), parts along dimension 0
- down_out: bfloat16 [32768, 256], P(('dp', 'space')), parts along dimension 0
- grad_features: bfloat16 [65536, 256], P(('dp', 'space')), parts along dimension 0
- conv_grad: float32 [108, 256, 256], P('dp', 'space'), parts along dimension 0
- down_grad: float32 [32, 256, 256], P('dp', 'space'), parts along dimension 0
The draws below stay inside these ranges and needn't reach their ends.
There are 4 independent parts, one for each index of `dp`. The reference program is written for one: setup_inputs(seed, part) draws one part's arguments, and reference() takes and returns one part's arrays. A program takes and returns all parts, laid end to end along the dimension named above; an argument that names none is the same for every part. Nothing has to cross between parts.
Inputs may be any that keep to these rules, and one draw needn't show every extreme that they name: Rows 0 to live_rows[d] - 1 of device d are occupied voxels, the others are empty; in every draw one device has 256 and one has 128. `halo_send`: entry p * 2 + s of device d's list is the occupied local row that d sends to device p in slot s, or -1 for an empty slot. `neighbors`: tap k = 9a + 3b + c stands for the offset (a - 1, b - 1, c - 1). A value below 256 is an occupied row of the same device; a value 256 + p * 2 + s is slot s of what device p sends to this device, never an empty slot; -1 means no neighbour. Tap 13 is the row itself; empty rows have -1 at every tap. `coarse_code`: -1 for empty rows; else (p * 2 + j) * 8 + o: coarse slot j toward device p, child offset o = 4a + 2b + c in the 2x2x2 cell; no two rows of a device share a value.
All inputs are finite; a program needn't handle non-finite values.
Results may differ from the reference program's by a relative error of at most 0.0055.
Values may be sent and summed in bfloat16 or wider, within the bound.
A program may use at most 128 MiB of HBM per device.

```python
import jax
import jax.numpy as jnp
from jax import lax

C = 256
ROWS = 256
HALO = 128
SLOT = 2
CSLOTS = 128
CSL = 2
ROWS_ALL = 16384
COARSE_ALL = 8192
GSCALE = 64
N_SPACE = 64


def make_tables(key):
    base_key = jax.random.fold_in(key, 31)
    key_list = jax.random.split(base_key, 9)
    shrink = jax.random.randint(key_list[0], (N_SPACE,), 0, ROWS // 2 + 1)
    live_count = (ROWS - shrink).astype(jnp.int32)
    full_dev = jax.random.randint(key_list[1], (), 0, N_SPACE)
    half_dev = (full_dev + 1 + jax.random.randint(key_list[2], (), 0, N_SPACE - 1)) % N_SPACE
    live_count = live_count.at[full_dev].set(ROWS).at[half_dev].set(ROWS // 2)
    slot_live = jax.random.randint(key_list[3], (N_SPACE, HALO), 0, 3) < 2
    chosen = jax.random.randint(key_list[4], (N_SPACE, HALO), 0, live_count[:, None])
    halo_list = jnp.where(slot_live, chosen, -1).astype(jnp.int32)
    halo_list = halo_list.at[N_SPACE - 1, SLOT - 1].set(0)
    halo_list = halo_list.at[full_dev, HALO - 1].set(ROWS - 1)
    incoming = halo_list.reshape(N_SPACE, N_SPACE, SLOT).transpose(1, 0, 2).reshape(N_SPACE, HALO) >= 0
    dice_roll = jax.random.randint(key_list[5], (27, N_SPACE, ROWS), 0, 100)
    local_pick = jax.random.randint(key_list[6], (27, N_SPACE, ROWS), 0, live_count[None, :, None])
    halo_pick = jax.random.randint(key_list[7], (27, N_SPACE, ROWS), 0, HALO)
    halo_ok = jnp.take_along_axis(jnp.broadcast_to(incoming[None], (27, N_SPACE, HALO)), halo_pick, axis=2)
    halo_ref = jnp.where(halo_ok, ROWS + halo_pick, -1)
    neighbor_table = jnp.where(dice_roll < 22, local_pick, jnp.where(dice_roll < 30, halo_ref, -1))
    row_ids = jnp.arange(ROWS, dtype=jnp.int32)
    row_live = row_ids[None, :] < live_count[:, None]
    neighbor_table = jnp.where(row_live[None], neighbor_table, -1)
    neighbor_table = neighbor_table.at[13].set(jnp.where(row_live, row_ids[None, :], -1))
    neighbor_table = neighbor_table.at[0, 0, 0].set(ROWS + HALO - 1)
    neighbor_table = neighbor_table.reshape(27, N_SPACE * ROWS).astype(jnp.int32)
    perm_keys = jax.random.split(key_list[8], N_SPACE)
    code_count = CSLOTS * 8

    def rotated(one_key):
        perm = jax.random.permutation(one_key, code_count)
        return ((perm + (code_count - 1 - perm[0])) % code_count)[:ROWS]
    code_table = jax.vmap(rotated)(perm_keys)
    code_table = jnp.where(row_live, code_table, -1).reshape(N_SPACE * ROWS).astype(jnp.int32)
    return (live_count, halo_list, neighbor_table, code_table)


def draw_live_rows(key, part):
    return make_tables(key)[0]


def draw_halo_send(key, part):
    return make_tables(key)[1]


def draw_neighbors(key, part):
    return make_tables(key)[2]


def draw_coarse_code(key, part):
    return make_tables(key)[3]


def raised(drawn, own_key, source, target, shards_of, factor):
    owner, partner = [(jnp.arange(drawn.shape[position]) // (drawn.shape[position] // shards_of)).reshape([-1 if axis == position else 1 for axis in range(drawn.ndim)]) for position in (source, target)]
    chosen = jax.random.permutation(own_key, shards_of)[partner]
    strong = (owner == chosen) | (owner == (partner + shards_of // 2) % shards_of)
    return jnp.where(strong, factor * drawn, drawn)


def levels(stream_key, dims, cuts, least, top_value):
    level, own = 1.0, jax.random.fold_in(stream_key, 6)
    for axis_at, blocks in cuts:
        draws = jnp.exp(jax.random.uniform(jax.random.fold_in(own, axis_at), (blocks,), jnp.float32, least / len(cuts), top_value / len(cuts)))
        level = level * jnp.repeat(draws, dims[axis_at] // blocks).reshape([-1 if axis == axis_at else 1 for axis in range(len(dims))])
    return level


def gaussian(key, dims, deviation, limit, cuts=(), kind=jnp.bfloat16):
    entries = jax.random.normal(key, dims, jnp.float32) * deviation
    if len(cuts) > 0:
        entries = levels(key, dims, cuts, -0.22, 0.18) * entries
    return jnp.clip(entries, min=-limit, max=limit).astype(kind)


def gaussian_with(key, dims, width, reach, pieces, heavy, held_as=jnp.bfloat16):
    array = width * jax.random.normal(key, dims, jnp.float32)
    if pieces:
        array = array * levels(key, dims, pieces, -0.22, 0.18)
    return jnp.clip(raised(array, jax.random.fold_in(key, 3), *heavy), -reach, reach).astype(held_as)


def setup_inputs(seed: int = 0, part: int = 0) -> dict:
    key_of = jax.random.split(jax.random.key(seed), 10)
    own_keys = jax.random.split(jax.random.fold_in(key_of[9], part), 10)
    features = gaussian_with(own_keys[0], (ROWS_ALL, C), 1.0, 16.0, ((0, 64),), (0, 1, 64, 4.0))
    conv_weight = gaussian(key_of[1], (27, C, C), (8 * C) ** -0.5, 0.125)
    down_weight = gaussian(key_of[2], (8, C, C), (2 * C) ** -0.5, 0.25)
    grad_conv = gaussian(own_keys[3], (ROWS_ALL, C), 1.0, 6.0, ((0, 64),))
    grad_down = gaussian(own_keys[4], (COARSE_ALL, C), 1.0, 6.0, ((0, 64),))
    live_rows = draw_live_rows(jax.random.fold_in(jax.random.fold_in(key_of[9], part), 71), part)
    halo_send = draw_halo_send(jax.random.fold_in(jax.random.fold_in(key_of[9], part), 71), part)
    neighbors = draw_neighbors(jax.random.fold_in(jax.random.fold_in(key_of[9], part), 71), part)
    coarse_code = draw_coarse_code(jax.random.fold_in(jax.random.fold_in(key_of[9], part), 71), part)
    return dict(features=features, conv_weight=conv_weight, down_weight=down_weight, grad_conv=grad_conv, grad_down=grad_down, live_rows=live_rows, halo_send=halo_send, neighbors=neighbors, coarse_code=coarse_code)


def reference(features, conv_weight, down_weight, grad_conv, grad_down, live_rows, halo_send, neighbors, coarse_code):
    row_total = ROWS * N_SPACE
    coarse_total = CSLOTS * N_SPACE
    channels = features.shape[1]
    row_ids = jnp.arange(row_total, dtype=jnp.int32)
    device_of = (row_ids // ROWS).astype(jnp.int32)
    local_id = row_ids % ROWS
    occupied = local_id < live_rows[device_of]
    halo_pos = jnp.clip(neighbors - ROWS, 0, HALO - 1)
    sender = (halo_pos // SLOT).astype(jnp.int32)
    column = (device_of[None, :] * SLOT + halo_pos % SLOT).astype(jnp.int32)
    sent_row = halo_send[sender, column]
    remote = jnp.where(sent_row >= 0, sender * ROWS + sent_row, row_total)
    source = jnp.where(neighbors < 0, row_total,
                       jnp.where(neighbors < ROWS, device_of[None, :] * ROWS + neighbors, remote)).astype(jnp.int32)
    zero_row = jnp.zeros((1, channels), jnp.bfloat16)
    padded = jnp.concatenate([features, zero_row], axis=0)

    def add_tap(running, tap_item):
        weight_tap, rows_at = tap_item
        picked = jnp.take(padded, rows_at, axis=0)
        return running + jnp.dot(picked, weight_tap, preferred_element_type=jnp.float32), None

    summed = lax.scan(add_tap, jnp.zeros((row_total, channels), jnp.float32), (conv_weight, source))[0]
    conv_out = jnp.where(occupied[:, None], summed, 0.0).astype(jnp.bfloat16)

    slot_id = coarse_code // 8
    owner = slot_id // CSL
    within = slot_id % CSL
    target = owner * CSLOTS + device_of * CSL + within
    child_pos = jnp.where(coarse_code >= 0, target * 8 + coarse_code % 8, coarse_total * 8).astype(jnp.int32)
    child_row = jnp.full((coarse_total * 8,), row_total, jnp.int32).at[child_pos].set(row_ids, mode="drop")
    conv_padded = jnp.concatenate([conv_out, zero_row], axis=0)
    children = jnp.take(conv_padded, child_row, axis=0).reshape(coarse_total, 8 * channels)
    down_flat = down_weight.reshape(8 * channels, channels)
    down_out = jnp.dot(children, down_flat, preferred_element_type=jnp.float32).astype(jnp.bfloat16)

    spread = lax.dot_general(grad_down, down_flat, (((1,), (1,)), ((), ())), preferred_element_type=jnp.float32)
    spread = jnp.concatenate([spread.reshape(coarse_total * 8, channels), jnp.zeros((1, channels), jnp.float32)], axis=0)
    from_down = jnp.take(spread, child_pos, axis=0)
    total_grad = jnp.where(occupied[:, None], grad_conv.astype(jnp.float32) + from_down, 0.0).astype(jnp.bfloat16)
    inverse_scale = 1.0 / GSCALE
    down_grad = lax.dot_general(children, grad_down, (((0,), (0,)), ((), ())), preferred_element_type=jnp.float32)
    down_grad = (down_grad * inverse_scale).reshape(8, channels, channels)

    def back_tap(carried, tap_item):
        weight_tap, rows_at = tap_item
        picked = jnp.take(padded, rows_at, axis=0)
        tap_grad = lax.dot_general(picked, total_grad, (((0,), (0,)), ((), ())), preferred_element_type=jnp.float32)
        pulled = lax.dot_general(total_grad, weight_tap, (((1,), (1,)), ((), ())), preferred_element_type=jnp.float32)
        return carried + jax.ops.segment_sum(pulled, rows_at, num_segments=row_total + 1), tap_grad

    start_grad = jnp.zeros((row_total + 1, channels), jnp.float32)
    input_grad, tap_grads = lax.scan(back_tap, start_grad, (conv_weight, source))
    conv_grad = tap_grads * inverse_scale
    grad_features = input_grad[:row_total].astype(jnp.bfloat16)
    return (conv_out, down_out, grad_features, conv_grad, down_grad)
```

```python
import jax
import jax.numpy as jnp
from jax import lax
from jax.experimental import pallas as pl
from jax.experimental.pallas import tpu as pltpu
from jax.sharding import PartitionSpec as P

MESH = pl.DeviceIdType.MESH
BF16, F32, I32 = jnp.bfloat16, jnp.float32, jnp.int32
NX, NZ, PEERS = 4, 8, 64
TAPS, GROUPS = 27, 9
CHUNKS = ((0, 4), (4, 7), (7, 9))


def mm(a, b):
    return jnp.dot(a, b, preferred_element_type=F32)


def mm_nt(a, b):
    return lax.dot_general(a, b, (((1,), (1,)), ((), ())), preferred_element_type=F32)


def mm_tn(a, b):
    return lax.dot_general(a, b, (((0,), (0,)), ((), ())), preferred_element_type=F32)


def onehot(mask):
    return jnp.where(mask, 1.0, 0.0).astype(BF16)


def iota(shape, dim):
    return lax.broadcasted_iota(I32, shape, dim)


def slot_row(q, kind, half):
    return 8 * (q // 2) + 2 * (2 * kind + q % 2) + half


def pack(first, second):
    row, q = iota((512, 128), 0), iota((512, 128), 1)
    total = jnp.zeros((512, 128), F32)
    for kind, rows in ((0, first), (1, second)):
        for half in range(2):
            place = onehot(row == slot_row(q, kind, half))
            total += mm(place, rows[:, half * 128 : half * 128 + 128])
    return total.reshape(PEERS, 8, 128).astype(BF16)


def unpack(slots, kind):
    q, row = iota((128, 512), 0), iota((128, 512), 1)
    flat = slots.astype(F32).reshape(512, 128).astype(BF16)
    return jnp.concatenate(
        [mm(onehot(row == slot_row(q, kind, half)), flat) for half in range(2)], axis=1
    )


def interleave(terms):
    a = [term.reshape(32, 8, 256) for term in terms]
    r = [pltpu.roll(value, 4, 1) for value in a]
    low = iota((32, 8, 256), 1) < 4
    first = jnp.concatenate(
        [jnp.where(low, a[0], r[1]), jnp.where(low, a[2], r[3])], axis=1
    )
    second = jnp.concatenate(
        [jnp.where(low, r[0], a[1]), jnp.where(low, r[2], a[3])], axis=1
    )
    return first.astype(BF16), second.astype(BF16)


def kernel(
    feat_ref,
    w_hbm,
    wd_hbm,
    gconv_ref,
    gdown_ref,
    live_ref,
    send_ref,
    nbr_ref,
    code_ref,
    conv_ref,
    down_ref,
    gfeat_ref,
    wg_ref,
    dg_ref,
    w_ref,
    wd_ref,
    oht,
    picked,
    cbo,
    total_ref,
    acc,
    ext_grad,
    a1_src,
    a1_dst,
    a2_src,
    a2_dst,
    part,
    got0,
    got1,
    got2,
    summed,
    got3,
    w_sem,
    a_ss,
    a_rs,
    s0,
    r0,
    s1,
    r1,
    s2,
    r2,
    s3,
    r3,
):
    me = lax.axis_index("space")
    x, z, core = me // 16, (me // 2) % NZ, me % 2
    x1, x2, x3 = x + 1 - 2 * (x % 2), (x + 2) % NX, 3 - x

    def device(xx, zz, cc):
        return {"space": (xx * NZ + zz) * 2 + cc}

    barrier = pltpu.get_barrier_semaphore()

    def greet(i, carry):
        pl.semaphore_signal(
            barrier, inc=1, device_id={"space": (me + i) % PEERS}, device_id_type=MESH
        )
        return carry

    lax.fori_loop(1, PEERS, greet, 0)
    w_copy = pltpu.make_async_copy(w_hbm, w_ref, w_sem.at[0])
    wd_copy = pltpu.make_async_copy(wd_hbm, wd_ref, w_sem.at[1])
    w_copy.start()
    wd_copy.start()

    def exchange(src, dst, which):
        def send(i, carry):
            peer = (me + i) % PEERS
            pltpu.make_async_remote_copy(
                src_ref=src.at[peer],
                dst_ref=dst.at[me],
                send_sem=a_ss.at[which],
                recv_sem=a_rs.at[which],
                device_id={"space": peer},
                device_id_type=MESH,
            ).start()
            return carry

        pltpu.make_async_copy(src.at[me], dst.at[me], a_rs.at[which]).start()
        lax.fori_loop(1, PEERS, send, 0)

    def exchange_wait(src, dst, which):
        pltpu.make_async_copy(src, dst, a_rs.at[which]).wait()

    def exchange_sent(src, dst, which):
        rest = pl.ds(0, PEERS - 1)
        pltpu.make_async_copy(src.at[rest], dst.at[rest], a_ss.at[which]).wait()

    feat = feat_ref[...]
    send_hot = onehot(iota((256, 128), 0) == send_ref[...])
    a1_src[...] = pack(mm_tn(send_hot, feat).astype(BF16), gdown_ref[...])
    pl.semaphore_wait(barrier, PEERS - 1)
    exchange(a1_src, a1_dst, 0)

    feat_t = feat.astype(F32).T.astype(BF16)
    acc[...] = jnp.zeros((256, 256), F32)
    picked[TAPS] = jnp.zeros((256, 256), BF16)
    oht[TAPS] = jnp.zeros((384, 256), BF16)
    w_copy.wait()

    def local_tap(k, carry):
        hot = onehot(iota((384, 256), 0) == nbr_ref[pl.ds(k, 1), :])
        oht[k] = hot
        own = mm(feat_t, hot[:256]).astype(BF16)
        picked[k] = own
        acc[...] += mm_tn(own, w_ref[k])
        return carry

    lax.fori_loop(0, TAPS, local_tap, 0)
    wd_copy.wait()

    exchange_wait(a1_src, a1_dst, 0)
    arrived = a1_dst[...]
    halo_t = unpack(arrived, 0).T.astype(BF16)
    coarse_back = unpack(arrived, 1).astype(BF16)
    code_row = code_ref[...]
    code_col = jnp.broadcast_to(code_row.astype(F32), (8, 256)).T[:, :1].astype(I32)
    from_down = jnp.zeros((256, 256), F32)
    for o in range(8):
        rows = mm(onehot(code_col == 8 * iota((256, 128), 1) + o), coarse_back).astype(BF16)
        cbo[o] = rows
        from_down += mm_nt(rows, wd_ref[o])
    occupied = iota((256, 256), 0) < live_ref[...]
    total = jnp.where(occupied, gconv_ref[...].astype(F32) + from_down, 0.0).astype(BF16)
    total_ref[...] = total

    def remote(src, dst, ss, rs, to):
        return pltpu.make_async_remote_copy(
            src_ref=src, dst_ref=dst, send_sem=ss, recv_sem=rs, device_id=to, device_id_type=MESH
        )

    def core_copy(g):
        return remote(part.at[1 - core, g], got0.at[g], s0.at[g], r0.at[g], device(x, z, 1 - core))

    za, zb = pl.ds(0, 4), pl.ds(4, 4)

    def x_copies(g):
        mine = part.at[core, g]
        there = got1.at[g]
        return [
            remote(mine.at[src, zs], there.at[slot, zs], s1.at[g, n], r1.at[g, n], device(to, z, core))
            for n, (src, slot, zs, to) in enumerate(
                ((x1, 0, za, x1), (x2, 1, za, x1), (x3, 0, zb, x3), (x2, 1, zb, x3))
            )
        ]

    def x_last(g):
        mine = part.at[core, g]
        there = got2.at[g]
        return [
            remote(mine.at[to, zs], there.at[zs], s2.at[g, n], r2.at[g, n], device(to, z, core))
            for n, (zs, to) in enumerate(((za, x3), (zb, x1)))
        ]

    def z_copies(c):
        span = pl.ds(CHUNKS[c][0], CHUNKS[c][1] - CHUNKS[c][0])
        out = []
        for i in range(1, NZ):
            to = (z + i) % NZ
            out.append(
                remote(
                    summed.at[span, to], got3.at[z, span], s3.at[c, i], r3.at[c, i], device(x, to, core)
                )
            )
        return out

    def give(g, terms):
        first, second = interleave(terms)
        part[0, g] = first.reshape(NX, NZ, 16, 256)
        part[1, g] = second.reshape(NX, NZ, 16, 256)
        core_copy(g).start()

    def conv_group(g):
        terms = []
        for t in range(4):
            k = 4 * g + t
            whole = picked[k] + mm(halo_t, oht[k, 256:384]).astype(BF16)
            terms.append(mm(whole, total_ref[...]))
        give(g, terms)

    def add(g, xx, zs, other):
        here = part[core, g, xx, zs].astype(F32) + other.astype(F32)
        part[core, g, xx, zs] = here.astype(BF16)

    def step1(g):
        core_copy(g).wait_recv()
        for xx in range(NX):
            part[core, g, xx] = (part[core, g, xx].astype(F32) + got0[g, xx].astype(F32)).astype(BF16)
        for copy in x_copies(g):
            copy.start()

    def step2(g):
        for copy in x_copies(g):
            copy.wait_recv()
        add(g, x3, za, got1[g, 1, za])
        add(g, x1, zb, got1[g, 1, zb])
        for copy in x_last(g):
            copy.start()
        add(g, x, za, got1[g, 0, za])
        add(g, x, zb, got1[g, 0, zb])

    def step3(g):
        for copy in x_last(g):
            copy.wait_recv()
        summed[g] = (part[core, g, x].astype(F32) + got2[g].astype(F32)).astype(BF16)

    def step4(c):
        for copy in z_copies(c):
            copy.start()

    def final(c):
        for copy in z_copies(c):
            copy.wait_recv()
        for g in range(*CHUNKS[c]):
            value = summed[g, z].astype(F32)
            for i in range(1, NZ):
                value += got3[(z + i) % NZ, g].astype(F32)
            value = (value * (1.0 / 64.0)).reshape(4, 4, 256)
            if g < 6:
                wg_ref[4 * g : 4 * g + 4] = value
            elif g == 6:
                wg_ref[24:27] = value[:3]
            else:
                dg_ref[4 * g - 28 : 4 * g - 24] = value

    def forward(lo, hi):
        def tap(k, carry):
            rows = mm(halo_t, oht[k, 256:384]).astype(BF16)
            acc[...] += mm_tn(rows, w_ref[k])
            return carry

        lax.fori_loop(lo, hi, tap, 0)

    def backward(lo, hi):
        def tap(k, carry):
            pulled = mm_nt(total_ref[...], w_ref[k]).astype(BF16)
            ext_grad[...] += mm(oht[k], pulled)
            return carry

        lax.fori_loop(lo, hi, tap, 0)

    conv_group(0)
    conv_group(1)
    step1(0)
    conv_group(2)
    step1(1)
    conv_group(3)
    step1(2)
    step2(0)
    conv_group(4)
    step1(3)
    step2(1)
    step3(0)
    conv_group(5)
    step1(4)
    step2(2)
    step3(1)
    conv_group(6)
    step1(5)
    step2(3)
    step3(2)
    forward(0, 14)
    step1(6)
    step2(4)
    step3(3)
    step4(0)
    forward(14, 27)
    conv_out = jnp.where(occupied, acc[...], 0.0).astype(BF16)
    conv_ref[...] = conv_out
    conv_t = conv_out.astype(F32).T.astype(BF16)
    give(7, [mm(conv_t, cbo[o]) for o in range(4)])
    step2(5)
    step3(4)
    give(8, [mm(conv_t, cbo[o]) for o in range(4, 8)])
    step1(7)
    step2(6)
    step3(5)
    coarse_part = jnp.zeros((128, 256), F32)
    for o in range(8):
        hot = onehot(code_row == 8 * iota((128, 256), 0) + o)
        coarse_part += mm(mm(hot, conv_out).astype(BF16), wd_ref[o])
    step1(8)
    step2(7)
    step3(6)
    step4(1)
    ext_grad[...] = jnp.zeros((384, 256), F32)
    backward(0, 14)
    step2(8)
    step3(7)
    backward(14, 27)
    a2_src[...] = pack(coarse_part.astype(BF16), ext_grad[256:384].astype(BF16))
    exchange(a2_src, a2_dst, 1)
    step3(8)
    step4(2)
    final(0)
    final(1)
    exchange_wait(a2_src, a2_dst, 1)
    arrived = a2_dst[...]
    down_ref[...] = unpack(arrived, 0).astype(BF16)
    returned = unpack(arrived, 1).astype(BF16)
    gfeat_ref[...] = (ext_grad[:256] + mm(send_hot, returned)).astype(BF16)
    final(2)
    exchange_sent(a1_src, a1_dst, 0)
    exchange_sent(a2_src, a2_dst, 1)
    for g in range(GROUPS):
        core_copy(g).wait_send()
        for copy in x_copies(g) + x_last(g):
            copy.wait_send()
    for c in range(len(CHUNKS)):
        for copy in z_copies(c):
            copy.wait_send()


def per_device(features, conv_weight, down_weight, grad_conv, grad_down, live_rows, halo_send, neighbors, coarse_code):
    vmem = pl.BlockSpec(memory_space=pltpu.VMEM)
    hbm = pl.BlockSpec(memory_space=pl.ANY)
    dma = pltpu.SemaphoreType.DMA
    return pl.pallas_call(
        kernel,
        out_shape=(
            jax.ShapeDtypeStruct((256, 256), BF16),
            jax.ShapeDtypeStruct((128, 256), BF16),
            jax.ShapeDtypeStruct((256, 256), BF16),
            jax.ShapeDtypeStruct((27, 4, 256), F32),
            jax.ShapeDtypeStruct((8, 4, 256), F32),
        ),
        in_specs=[vmem, hbm, hbm, vmem, vmem, vmem, vmem, vmem, vmem],
        out_specs=[vmem] * 5,
        scratch_shapes=[
            pltpu.VMEM((27, 256, 256), BF16),
            pltpu.VMEM((8, 256, 256), BF16),
            pltpu.VMEM((28, 384, 256), BF16),
            pltpu.VMEM((28, 256, 256), BF16),
            pltpu.VMEM((8, 256, 256), BF16),
            pltpu.VMEM((256, 256), BF16),
            pltpu.VMEM((256, 256), F32),
            pltpu.VMEM((384, 256), F32),
            pltpu.VMEM((PEERS, 8, 128), BF16),
            pltpu.VMEM((PEERS, 8, 128), BF16),
            pltpu.VMEM((PEERS, 8, 128), BF16),
            pltpu.VMEM((PEERS, 8, 128), BF16),
            pltpu.VMEM((2, GROUPS, NX, NZ, 16, 256), BF16),
            pltpu.VMEM((GROUPS, NX, NZ, 16, 256), BF16),
            pltpu.VMEM((GROUPS, 2, NZ, 16, 256), BF16),
            pltpu.VMEM((GROUPS, NZ, 16, 256), BF16),
            pltpu.VMEM((GROUPS, NZ, 16, 256), BF16),
            pltpu.VMEM((NZ, GROUPS, 16, 256), BF16),
            dma((2,)),
            dma((2,)),
            dma((2,)),
            dma((GROUPS,)),
            dma((GROUPS,)),
            dma((GROUPS, 4)),
            dma((GROUPS, 4)),
            dma((GROUPS, 2)),
            dma((GROUPS, 2)),
            dma((3, NZ)),
            dma((3, NZ)),
        ],
        compiler_params=pltpu.CompilerParams(
            collective_id=0, has_side_effects=True, vmem_limit_bytes=56 * 2**20
        ),
        cost_estimate=pl.CostEstimate(flops=7 * 10**9, bytes_accessed=6 * 10**6, transcendentals=0),
    )(
        features,
        conv_weight,
        down_weight,
        grad_conv,
        grad_down,
        live_rows.reshape(1, 1),
        halo_send,
        neighbors,
        coarse_code.reshape(1, 256),
    )


def solution(mesh):
    rows = P(("dp", "space"), None)
    return jax.shard_map(
        per_device,
        mesh=mesh,
        in_specs=(rows, P(), P(), rows, rows, P(("dp", "space")), rows, P(None, ("dp", "space")), P(("dp", "space"))),
        out_specs=(rows, rows, rows, P("dp", "space", None), P("dp", "space", None)),
        check_vma=False,
    )
```

```python
import jax
import jax.numpy as jnp
from jax import lax
from jax.experimental import pallas as pl
from jax.experimental.pallas import tpu as pltpu
from jax.sharding import PartitionSpec as P

MESH = pl.DeviceIdType.MESH
BF16, F32, I32 = jnp.bfloat16, jnp.float32, jnp.int32
NX, NZ, PEERS = 4, 8, 64
TAPS, GROUPS = 27, 9
CHUNKS = ((0, 4), (4, 7), (7, 9))


def mm(a, b):
    return jnp.dot(a, b, preferred_element_type=F32)


def mm_nt(a, b):
    return lax.dot_general(a, b, (((1,), (1,)), ((), ())), preferred_element_type=F32)


def mm_tn(a, b):
    return lax.dot_general(a, b, (((0,), (0,)), ((), ())), preferred_element_type=F32)


def onehot(mask):
    return jnp.where(mask, 1.0, 0.0).astype(BF16)


def iota(shape, dim):
    return lax.broadcasted_iota(I32, shape, dim)


def tap(k):
    return slice(256 * k, 256 * k + 256)


def slot_row(q, kind, half):
    return 8 * (q // 2) + 2 * (2 * kind + q % 2) + half


def pack(first, second):
    row, q = iota((512, 128), 0), iota((512, 128), 1)
    total = jnp.zeros((512, 128), F32)
    for kind, rows in ((0, first), (1, second)):
        for half in range(2):
            place = onehot(row == slot_row(q, kind, half))
            total += mm(place, rows[:, half * 128 : half * 128 + 128])
    return total.reshape(PEERS, 8, 128).astype(BF16)


def unpack(slots, kind):
    q, row = iota((128, 512), 0), iota((128, 512), 1)
    flat = slots.astype(F32).reshape(512, 128).astype(BF16)
    return jnp.concatenate(
        [mm(onehot(row == slot_row(q, kind, half)), flat) for half in range(2)], axis=1
    )


def interleave(terms):
    a = [term.reshape(32, 8, 256) for term in terms]
    r = [pltpu.roll(value, 4, 1) for value in a]
    low = iota((32, 8, 256), 1) < 4
    first = jnp.concatenate(
        [jnp.where(low, a[0], r[1]), jnp.where(low, a[2], r[3])], axis=1
    )
    second = jnp.concatenate(
        [jnp.where(low, r[0], a[1]), jnp.where(low, r[2], a[3])], axis=1
    )
    return first.astype(BF16), second.astype(BF16)


def kernel(
    feat_ref,
    w_hbm,
    wd_hbm,
    gconv_ref,
    gdown_ref,
    live_ref,
    send_ref,
    nbr_ref,
    code_ref,
    conv_ref,
    down_ref,
    gfeat_ref,
    wg_ref,
    dg_ref,
    w_ref,
    wd_ref,
    wt,
    oht,
    picked,
    pulled,
    cbo,
    total_ref,
    ext_grad,
    a1_src,
    a1_dst,
    a2_src,
    a2_dst,
    part,
    got0,
    got1,
    got2,
    summed,
    got3,
    w_sem,
    a_ss,
    a_rs,
    s0,
    r0,
    s1,
    r1,
    s2,
    r2,
    s3,
    r3,
):
    me = lax.axis_index("space")
    x, z, core = me // 16, (me // 2) % NZ, me % 2
    x1, x2, x3 = x + 1 - 2 * (x % 2), (x + 2) % NX, 3 - x

    def device(xx, zz, cc):
        return {"space": (xx * NZ + zz) * 2 + cc}

    barrier = pltpu.get_barrier_semaphore()

    def greet(i, carry):
        pl.semaphore_signal(
            barrier, inc=1, device_id={"space": (me + i) % PEERS}, device_id_type=MESH
        )
        return carry

    lax.fori_loop(1, PEERS, greet, 0)
    w_copy = pltpu.make_async_copy(w_hbm, w_ref, w_sem.at[0])
    wd_copy = pltpu.make_async_copy(wd_hbm, wd_ref, w_sem.at[1])
    w_copy.start()
    wd_copy.start()

    def exchange(src, dst, which):
        def send(i, carry):
            peer = (me + i) % PEERS
            pltpu.make_async_remote_copy(
                src_ref=src.at[peer],
                dst_ref=dst.at[me],
                send_sem=a_ss.at[which],
                recv_sem=a_rs.at[which],
                device_id={"space": peer},
                device_id_type=MESH,
            ).start()
            return carry

        pltpu.make_async_copy(src.at[me], dst.at[me], a_rs.at[which]).start()
        lax.fori_loop(1, PEERS, send, 0)

    def exchange_wait(src, dst, which):
        pltpu.make_async_copy(src, dst, a_rs.at[which]).wait()

    def exchange_sent(src, dst, which):
        rest = pl.ds(0, PEERS - 1)
        pltpu.make_async_copy(src.at[rest], dst.at[rest], a_ss.at[which]).wait()

    feat = feat_ref[...]
    send_hot = onehot(iota((256, 128), 0) == send_ref[...])
    a1_src[...] = pack(mm_tn(send_hot, feat).astype(BF16), gdown_ref[...])
    feat_t = feat.astype(F32).T.astype(BF16)
    source = iota((384, 256), 0)
    for k in range(TAPS):
        oht[:, tap(k)] = onehot(source == nbr_ref[k : k + 1, :])
    for k in range(TAPS):
        picked[tap(k)] = mm(feat_t, oht[:256, tap(k)]).astype(BF16)
    pl.semaphore_wait(barrier, PEERS - 1)
    exchange(a1_src, a1_dst, 0)
    w_copy.wait()
    for k in range(TAPS):
        wt[:, tap(k)] = w_ref[k].T
    wd_copy.wait()

    exchange_wait(a1_src, a1_dst, 0)
    arrived = a1_dst[...]
    halo_t = unpack(arrived, 0).T.astype(BF16)
    coarse_back = unpack(arrived, 1).astype(BF16)
    code_row = code_ref[...]
    code_col = jnp.broadcast_to(code_row.astype(F32), (8, 256)).T[:, :1].astype(I32)
    from_down = jnp.zeros((256, 256), F32)
    for o in range(8):
        rows = mm(onehot(code_col == 8 * iota((256, 128), 1) + o), coarse_back).astype(BF16)
        cbo[o] = rows
        from_down += mm_nt(rows, wd_ref[o])
    occupied = iota((256, 256), 0) < live_ref[...]
    total = jnp.where(occupied, gconv_ref[...].astype(F32) + from_down, 0.0).astype(BF16)
    total_ref[...] = total

    def remote(src, dst, ss, rs, to):
        return pltpu.make_async_remote_copy(
            src_ref=src, dst_ref=dst, send_sem=ss, recv_sem=rs, device_id=to, device_id_type=MESH
        )

    def core_copy(g):
        return remote(part.at[1 - core, g], got0.at[g], s0.at[g], r0.at[g], device(x, z, 1 - core))

    za, zb = pl.ds(0, 4), pl.ds(4, 4)

    def x_copies(g):
        mine = part.at[core, g]
        there = got1.at[g]
        return [
            remote(mine.at[src, zs], there.at[slot, zs], s1.at[g, n], r1.at[g, n], device(to, z, core))
            for n, (src, slot, zs, to) in enumerate(
                ((x1, 0, za, x1), (x2, 1, za, x1), (x3, 0, zb, x3), (x2, 1, zb, x3))
            )
        ]

    def x_last(g):
        mine = part.at[core, g]
        there = got2.at[g]
        return [
            remote(mine.at[to, zs], there.at[zs], s2.at[g, n], r2.at[g, n], device(to, z, core))
            for n, (zs, to) in enumerate(((za, x3), (zb, x1)))
        ]

    def z_copies(c):
        span = pl.ds(CHUNKS[c][0], CHUNKS[c][1] - CHUNKS[c][0])
        out = []
        for i in range(1, NZ):
            to = (z + i) % NZ
            out.append(
                remote(
                    summed.at[span, to], got3.at[z, span], s3.at[c, i], r3.at[c, i], device(x, to, core)
                )
            )
        return out

    def give(g, terms):
        first, second = interleave(terms)
        part[0, g] = first.reshape(NX, NZ, 16, 256)
        part[1, g] = second.reshape(NX, NZ, 16, 256)
        core_copy(g).start()

    def conv_group(g):
        taps = range(4 * g, min(4 * g + 4, TAPS))
        for k in taps:
            picked[tap(k)] += mm(halo_t, oht[256:, tap(k)]).astype(BF16)
        terms = [mm(picked[tap(k)], total_ref[...]) for k in taps]
        give(g, terms + [jnp.zeros((256, 256), F32)] * (4 - len(terms)))

    def add(g, xx, zs, other):
        here = part[core, g, xx, zs].astype(F32) + other.astype(F32)
        part[core, g, xx, zs] = here.astype(BF16)

    def step1(g):
        core_copy(g).wait_recv()
        for xx in range(NX):
            part[core, g, xx] = (part[core, g, xx].astype(F32) + got0[g, xx].astype(F32)).astype(BF16)
        for copy in x_copies(g):
            copy.start()

    def step2(g):
        for copy in x_copies(g):
            copy.wait_recv()
        add(g, x3, za, got1[g, 1, za])
        add(g, x1, zb, got1[g, 1, zb])
        for copy in x_last(g):
            copy.start()
        add(g, x, za, got1[g, 0, za])
        add(g, x, zb, got1[g, 0, zb])

    def step3(g):
        for copy in x_last(g):
            copy.wait_recv()
        summed[g] = (part[core, g, x].astype(F32) + got2[g].astype(F32)).astype(BF16)

    def step4(c):
        for copy in z_copies(c):
            copy.start()

    def final(c):
        for copy in z_copies(c):
            copy.wait_recv()
        for g in range(*CHUNKS[c]):
            value = summed[g, z].astype(F32)
            for i in range(1, NZ):
                value += got3[(z + i) % NZ, g].astype(F32)
            value = (value * (1.0 / 64.0)).reshape(4, 4, 256)
            if g < 6:
                wg_ref[4 * g : 4 * g + 4] = value
            elif g == 6:
                wg_ref[24:27] = value[:3]
            else:
                dg_ref[4 * g - 28 : 4 * g - 24] = value

    def pull(lo, hi):
        for k in range(lo, hi):
            pulled[tap(k)] = mm(total_ref[...], wt[:, tap(k)]).astype(BF16)

    def scatter(lo, hi):
        span = slice(256 * lo, 256 * hi)
        return mm(oht[:, span], pulled[span])

    conv_group(0)
    conv_group(1)
    step1(0)
    conv_group(2)
    step1(1)
    conv_group(3)
    step1(2)
    step2(0)
    conv_group(4)
    step1(3)
    step2(1)
    step3(0)
    conv_group(5)
    step1(4)
    step2(2)
    step3(1)
    conv_group(6)
    step1(5)
    step2(3)
    step3(2)
    summed_t = mm(wt[...], picked[...])
    step1(6)
    step2(4)
    step3(3)
    step4(0)
    conv_out = jnp.where(occupied, summed_t.T, 0.0).astype(BF16)
    conv_ref[...] = conv_out
    conv_t = conv_out.T
    give(7, [mm(conv_t, cbo[o]) for o in range(4)])
    step2(5)
    step3(4)
    give(8, [mm(conv_t, cbo[o]) for o in range(4, 8)])
    step1(7)
    step2(6)
    step3(5)
    coarse_part = jnp.zeros((128, 256), F32)
    for o in range(8):
        hot = onehot(code_row == 8 * iota((128, 256), 0) + o)
        coarse_part += mm(mm(hot, conv_out).astype(BF16), wd_ref[o])
    step1(8)
    step2(7)
    step3(6)
    step4(1)
    pull(0, 14)
    ext_grad[...] = scatter(0, 14)
    step2(8)
    step3(7)
    pull(14, 27)
    ext_grad[...] += scatter(14, 27)
    a2_src[...] = pack(coarse_part.astype(BF16), ext_grad[256:384].astype(BF16))
    exchange(a2_src, a2_dst, 1)
    step3(8)
    step4(2)
    final(0)
    final(1)
    exchange_wait(a2_src, a2_dst, 1)
    arrived = a2_dst[...]
    down_ref[...] = unpack(arrived, 0).astype(BF16)
    returned = unpack(arrived, 1).astype(BF16)
    gfeat_ref[...] = (ext_grad[:256] + mm(send_hot, returned)).astype(BF16)
    final(2)
    exchange_sent(a1_src, a1_dst, 0)
    exchange_sent(a2_src, a2_dst, 1)
    for g in range(GROUPS):
        core_copy(g).wait_send()
        for copy in x_copies(g) + x_last(g):
            copy.wait_send()
    for c in range(len(CHUNKS)):
        for copy in z_copies(c):
            copy.wait_send()


def place(*refs):
    for held, out in zip(refs[:5], refs[5:]):
        out[...] = held[...]


def per_device(features, conv_weight, down_weight, grad_conv, grad_down, live_rows, halo_send, neighbors, coarse_code):
    vmem = pl.BlockSpec(memory_space=pltpu.VMEM)
    hbm = pl.BlockSpec(memory_space=pl.ANY)
    dma = pltpu.SemaphoreType.DMA
    results = pl.pallas_call(
        kernel,
        out_shape=(
            jax.ShapeDtypeStruct((256, 256), BF16),
            jax.ShapeDtypeStruct((128, 256), BF16),
            jax.ShapeDtypeStruct((256, 256), BF16),
            jax.ShapeDtypeStruct((27, 4, 256), F32),
            jax.ShapeDtypeStruct((8, 4, 256), F32),
        ),
        in_specs=[vmem, hbm, hbm, vmem, vmem, vmem, vmem, vmem, vmem],
        out_specs=[vmem] * 5,
        scratch_shapes=[
            pltpu.VMEM((27, 256, 256), BF16),
            pltpu.VMEM((8, 256, 256), BF16),
            pltpu.VMEM((256, 256 * TAPS), BF16),
            pltpu.VMEM((384, 256 * TAPS), BF16),
            pltpu.VMEM((256 * TAPS, 256), BF16),
            pltpu.VMEM((256 * TAPS, 256), BF16),
            pltpu.VMEM((8, 256, 256), BF16),
            pltpu.VMEM((256, 256), BF16),
            pltpu.VMEM((384, 256), F32),
            pltpu.VMEM((PEERS, 8, 128), BF16),
            pltpu.VMEM((PEERS, 8, 128), BF16),
            pltpu.VMEM((PEERS, 8, 128), BF16),
            pltpu.VMEM((PEERS, 8, 128), BF16),
            pltpu.VMEM((2, GROUPS, NX, NZ, 16, 256), BF16),
            pltpu.VMEM((GROUPS, NX, NZ, 16, 256), BF16),
            pltpu.VMEM((GROUPS, 2, NZ, 16, 256), BF16),
            pltpu.VMEM((GROUPS, NZ, 16, 256), BF16),
            pltpu.VMEM((GROUPS, NZ, 16, 256), BF16),
            pltpu.VMEM((NZ, GROUPS, 16, 256), BF16),
            dma((2,)),
            dma((2,)),
            dma((2,)),
            dma((GROUPS,)),
            dma((GROUPS,)),
            dma((GROUPS, 4)),
            dma((GROUPS, 4)),
            dma((GROUPS, 2)),
            dma((GROUPS, 2)),
            dma((3, NZ)),
            dma((3, NZ)),
        ],
        compiler_params=pltpu.CompilerParams(
            collective_id=0, has_side_effects=True, vmem_limit_bytes=56 * 2**20
        ),
        cost_estimate=pl.CostEstimate(flops=7 * 10**9, bytes_accessed=6 * 10**6, transcendentals=0),
    )(
        features,
        conv_weight,
        down_weight,
        grad_conv,
        grad_down,
        live_rows.reshape(1, 1),
        halo_send,
        neighbors,
        coarse_code.reshape(1, 256),
    )
    return pl.pallas_call(
        place,
        out_shape=tuple(jax.ShapeDtypeStruct(r.shape, r.dtype) for r in results),
        in_specs=[vmem] * 5,
        out_specs=[vmem] * 5,
    )(*results)


def solution(mesh):
    rows = P(("dp", "space"), None)
    return jax.shard_map(
        per_device,
        mesh=mesh,
        in_specs=(rows, P(), P(), rows, rows, P(("dp", "space")), rows, P(None, ("dp", "space")), P(("dp", "space"))),
        out_specs=(rows, rows, rows, P("dp", "space", None), P("dp", "space", None)),
        check_vma=False,
    )
```

```python
import jax
import jax.numpy as jnp
from jax import lax
from jax.experimental import pallas as pl
from jax.experimental.pallas import tpu as pltpu
from jax.sharding import PartitionSpec as P

MESH = pl.DeviceIdType.MESH
BF16, F32, I32 = jnp.bfloat16, jnp.float32, jnp.int32
NX, NZ = 4, 8
TAPS, GROUPS = 27, 9
CHUNKS = ((0, 1), (1, 3), (3, 5), (5, 7), (7, 9))
PARTS = len(CHUNKS)


def mm(a, b):
    return jnp.dot(a, b, preferred_element_type=F32)


def mm_nt(a, b):
    return lax.dot_general(a, b, (((1,), (1,)), ((), ())), preferred_element_type=F32)


def mm_tn(a, b):
    return lax.dot_general(a, b, (((0,), (0,)), ((), ())), preferred_element_type=F32)


def onehot(mask):
    return jnp.where(mask, 1.0, 0.0).astype(BF16)


def iota(shape, dim):
    return lax.broadcasted_iota(I32, shape, dim)


def tap(k):
    return slice(256 * k, 256 * k + 256)


def slot_row(q, kind, half, arriving):
    peer = q // 2
    line, column = (peer // 2) % NZ, 2 * (peer // 16) + peer % 2
    slot = 8 * column + line if arriving else 8 * line + column
    return 8 * slot + 2 * (2 * kind + q % 2) + half


def pack(first, second):
    row, q = iota((512, 128), 0), iota((512, 128), 1)
    total = jnp.zeros((512, 128), F32)
    for kind, rows in ((0, first), (1, second)):
        for half in range(2):
            place = onehot(row == slot_row(q, kind, half, False))
            total += mm(place, rows[:, half * 128 : half * 128 + 128])
    return total.reshape(8, 8, 8, 128).astype(BF16)


def unpack(slots, kind):
    q, row = iota((128, 512), 0), iota((128, 512), 1)
    flat = slots.astype(F32).reshape(512, 128).astype(BF16)
    return jnp.concatenate(
        [mm(onehot(row == slot_row(q, kind, half, True)), flat) for half in range(2)], axis=1
    )


def interleave(terms):
    a = [term.reshape(32, 8, 256) for term in terms]
    r = [pltpu.roll(value, 4, 1) for value in a]
    low = iota((32, 8, 256), 1) < 4
    first = jnp.concatenate(
        [jnp.where(low, a[0], r[1]), jnp.where(low, a[2], r[3])], axis=1
    )
    second = jnp.concatenate(
        [jnp.where(low, r[0], a[1]), jnp.where(low, r[2], a[3])], axis=1
    )
    return first, second


def kernel(
    feat_ref,
    w_hbm,
    wd_hbm,
    gconv_ref,
    gdown_ref,
    live_ref,
    send_ref,
    nbr_ref,
    code_ref,
    conv_ref,
    down_ref,
    gfeat_ref,
    wg_ref,
    dg_ref,
    w_ref,
    wd_ref,
    wt,
    oht,
    picked,
    pulled,
    cbo,
    total_ref,
    ext_grad,
    a1_src,
    a1_mid,
    a1_dst,
    a2_src,
    a2_mid,
    a2_dst,
    mine,
    give0,
    got0,
    give1,
    got1,
    give2,
    got2,
    give3,
    got3,
    w_sem,
    a_ss,
    a_rs,
    r_ss,
    r_rs,
    z_ss,
    z_rs,
):
    me = lax.axis_index("space")
    x, z, core = me // 16, (me // 2) % NZ, me % 2
    x1, x2, x3 = x + 1 - 2 * (x % 2), (x + 2) % NX, 3 - x

    column = 2 * x + core

    def device(xx, zz, cc):
        return {"space": (xx * NZ + zz) * 2 + cc}

    def in_line(i):
        return (z + i) % NZ

    def in_plane(i):
        return (column + i) % 8

    barrier = pltpu.get_barrier_semaphore()
    for i in range(1, 8):
        for to in (device(x, in_line(i), core), device(in_plane(i) // 2, z, in_plane(i) % 2)):
            pl.semaphore_signal(barrier, inc=1, device_id=to, device_id_type=MESH)
    w_copy = pltpu.make_async_copy(w_hbm, w_ref, w_sem.at[0])
    wd_copy = pltpu.make_async_copy(wd_hbm, wd_ref, w_sem.at[1])
    w_copy.start()
    wd_copy.start()

    def remote(src, dst, ss, rs, to):
        return pltpu.make_async_remote_copy(
            src_ref=src, dst_ref=dst, send_sem=ss, recv_sem=rs, device_id=to, device_id_type=MESH
        )

    def line_start(src, mid, which):
        ss, rs = a_ss.at[which, 0], a_rs.at[which, 0]
        for i in range(1, 8):
            to = in_line(i)
            remote(src.at[to], mid.at[z], ss, rs, device(x, to, core)).start()
        pltpu.make_async_copy(src.at[z], mid.at[z], rs).start()

    def line_wait(src, mid, which):
        pltpu.make_async_copy(src, mid, a_rs.at[which, 0]).wait()

    def plane_start(mid, dst, which):
        ss, rs = a_ss.at[which, 1], a_rs.at[which, 1]
        for i in range(1, 8):
            to = in_plane(i)
            remote(mid.at[:, to], dst.at[column], ss, rs, device(to // 2, z, to % 2)).start()
        pltpu.make_async_copy(mid.at[:, column], dst.at[column], rs).start()

    def plane_wait(mid, dst, which):
        pltpu.make_async_copy(mid, dst, a_rs.at[which, 1]).wait()

    def exchange_sent(buffer, which):
        rest = buffer.at[pl.ds(0, 7)]
        for phase in range(2):
            pltpu.make_async_copy(rest, rest, a_ss.at[which, phase]).wait()

    feat = feat_ref[...]
    send_hot = onehot(iota((256, 128), 0) == send_ref[...])
    a1_src[...] = pack(mm_tn(send_hot, feat).astype(BF16), gdown_ref[...])
    pl.semaphore_wait(barrier, 14)
    line_start(a1_src, a1_mid, 0)
    feat_t = feat.astype(F32).T.astype(BF16)
    source = iota((384, 256), 0)
    for k in range(TAPS):
        oht[:, tap(k)] = onehot(source == nbr_ref[k : k + 1, :])
    line_wait(a1_src, a1_mid, 0)
    plane_start(a1_mid, a1_dst, 0)
    for k in range(TAPS):
        picked[tap(k)] = mm(feat_t, oht[:256, tap(k)]).astype(BF16)
    w_copy.wait()
    for k in range(TAPS):
        wt[:, tap(k)] = w_ref[k].T
    wd_copy.wait()

    plane_wait(a1_mid, a1_dst, 0)
    arrived = a1_dst[...]
    halo_t = unpack(arrived, 0).T.astype(BF16)
    coarse_back = unpack(arrived, 1).astype(BF16)
    code_row = code_ref[...]
    code_col = jnp.broadcast_to(code_row.astype(F32), (8, 256)).T[:, :1].astype(I32)
    from_down = jnp.zeros((256, 256), F32)
    for o in range(8):
        rows = mm(onehot(code_col == 8 * iota((256, 128), 1) + o), coarse_back).astype(BF16)
        cbo[o] = rows
        from_down += mm_nt(rows, wd_ref[o])
    occupied = iota((256, 256), 0) < live_ref[0]
    total = jnp.where(occupied, gconv_ref[...].astype(F32) + from_down, 0.0).astype(BF16)
    total_ref[...] = total

    near, far = (x1, x3), (x3, x1)

    def span(c):
        return pl.ds(CHUNKS[c][0], CHUNKS[c][1] - CHUNKS[c][0])

    def copies(c, step):
        s = span(c)
        if step == 0:
            return [remote(give0.at[s], got0.at[s], r_ss.at[c, 0, 0], r_rs.at[c, 0, 0], device(x, z, 1 - core))]
        if step == 3:
            return [
                remote(give3.at[in_line(i), s], got3.at[z, s], z_ss.at[c, i], z_rs.at[c, i], device(x, in_line(i), core))
                for i in range(1, NZ)
            ]
        give, got, to = (give1, got1, near) if step == 1 else (give2, got2, far)
        return [
            remote(give.at[h, s], got.at[h, s], r_ss.at[c, step, h], r_rs.at[c, step, h], device(to[h], z, core))
            for h in range(2)
        ]

    def send(c, step):
        for copy in copies(c, step):
            copy.start()

    def receive(c, step):
        for copy in copies(c, step):
            copy.wait_recv()

    def give(g, terms):
        first, second = interleave(terms)
        own = jnp.where(core == 0, first, second)
        other = jnp.where(core == 0, second, first).astype(BF16)
        for h in range(2):
            half = slice(128 * h, 128 * h + 128)
            mine[g, h] = own[:, :, half].reshape(NX, NZ, 16, 128)
            give0[g, h] = other[:, :, half].reshape(NX, NZ, 16, 128)

    def step1(c):
        s = span(c)
        receive(c, 0)
        for h in range(2):
            for i, xx in enumerate((near[h], x2)):
                give1[h, s, i] = (mine[s, h, xx] + got0[s, h, xx].astype(F32)).astype(BF16)
        send(c, 1)
        for h in range(2):
            for xx in (x, far[h]):
                mine[s, h, xx] += got0[s, h, xx].astype(F32)

    def step2(c):
        s = span(c)
        receive(c, 1)
        for h in range(2):
            give2[h, s] = (mine[s, h, far[h]] + got1[h, s, 1].astype(F32)).astype(BF16)
        send(c, 2)
        for h in range(2):
            mine[s, h, x] += got1[h, s, 0].astype(F32)

    def step3(c):
        s = span(c)
        receive(c, 2)
        for h in range(2):
            value = mine[s, h, x] + got2[h, s].astype(F32)
            mine[s, h, x] = value
            for zz in range(NZ):
                give3[zz, s, :, 128 * h : 128 * h + 128] = value[:, zz].astype(BF16)
        send(c, 3)

    def final(c):
        receive(c, 3)
        for g in range(*CHUNKS[c]):
            value = jnp.concatenate([mine[g, h, x, z] for h in range(2)], axis=1)
            for i in range(1, NZ):
                value += got3[in_line(i), g].astype(F32)
            value = (value * (1.0 / 64.0)).reshape(4, 4, 256)
            if g < 6:
                wg_ref[4 * g : 4 * g + 4] = value
            elif g == 6:
                wg_ref[24:27] = value[:3]
            else:
                dg_ref[4 * g - 28 : 4 * g - 24] = value

    def conv_group(g):
        taps = range(4 * g, min(4 * g + 4, TAPS))
        for k in taps:
            picked[tap(k)] += mm(halo_t, oht[256:, tap(k)]).astype(BF16)
        terms = [mm(picked[tap(k)], total_ref[...]) for k in taps]
        give(g, terms + [jnp.zeros((256, 256), F32)] * (4 - len(terms)))

    def pull(lo, hi):
        for k in range(lo, hi):
            pulled[tap(k)] = mm(total_ref[...], wt[:, tap(k)]).astype(BF16)

    def scatter(lo, hi):
        span = slice(256 * lo, 256 * hi)
        return mm(oht[:, span], pulled[span])

    for c in range(4):
        for g in range(*CHUNKS[c]):
            conv_group(g)
        send(c, 0)
        if c > 0:
            step1(c - 1)
    summed_t = mm(wt[...], picked[...])
    step1(3)
    conv_out = jnp.where(occupied, summed_t.T, 0.0).astype(BF16)
    conv_ref[...] = conv_out
    conv_t = conv_out.T
    give(7, [mm(conv_t, cbo[o]) for o in range(4)])
    give(8, [mm(conv_t, cbo[o]) for o in range(4, 8)])
    send(4, 0)
    step2(0)
    coarse_part = jnp.zeros((128, 256), F32)
    for o in range(8):
        hot = onehot(code_row == 8 * iota((128, 256), 0) + o)
        coarse_part += mm(mm(hot, conv_out).astype(BF16), wd_ref[o])
    step1(4)
    pull(0, 27)
    step2(1)
    ext_grad[...] = scatter(0, 27)
    a2_src[...] = pack(coarse_part.astype(BF16), ext_grad[256:384].astype(BF16))
    line_start(a2_src, a2_mid, 1)
    step3(0)
    step2(2)
    step3(1)
    line_wait(a2_src, a2_mid, 1)
    plane_start(a2_mid, a2_dst, 1)
    step2(3)
    step3(2)
    final(0)
    step2(4)
    step3(3)
    final(1)
    step3(4)
    plane_wait(a2_mid, a2_dst, 1)
    arrived = a2_dst[...]
    down_ref[...] = unpack(arrived, 0).astype(BF16)
    returned = unpack(arrived, 1).astype(BF16)
    gfeat_ref[...] = (ext_grad[:256] + mm(send_hot, returned)).astype(BF16)
    final(2)
    final(3)
    final(4)
    exchange_sent(a1_src, 0)
    exchange_sent(a2_src, 1)
    for c in range(PARTS):
        for step in range(4):
            for copy in copies(c, step):
                copy.wait_send()


def place(*refs):
    for held, out in zip(refs[:5], refs[5:]):
        out[...] = held[...]


def per_device(features, conv_weight, down_weight, grad_conv, grad_down, live_rows, halo_send, neighbors, coarse_code):
    vmem = pl.BlockSpec(memory_space=pltpu.VMEM)
    hbm = pl.BlockSpec(memory_space=pl.ANY)
    dma = pltpu.SemaphoreType.DMA
    results = pl.pallas_call(
        kernel,
        out_shape=(
            jax.ShapeDtypeStruct((256, 256), BF16),
            jax.ShapeDtypeStruct((128, 256), BF16),
            jax.ShapeDtypeStruct((256, 256), BF16),
            jax.ShapeDtypeStruct((27, 4, 256), F32),
            jax.ShapeDtypeStruct((8, 4, 256), F32),
        ),
        in_specs=[vmem, hbm, hbm, vmem, vmem, pl.BlockSpec(memory_space=pltpu.SMEM), vmem, vmem, vmem],
        out_specs=[vmem] * 5,
        scratch_shapes=[
            pltpu.VMEM((27, 256, 256), BF16),
            pltpu.VMEM((8, 256, 256), BF16),
            pltpu.VMEM((256, 256 * TAPS), BF16),
            pltpu.VMEM((384, 256 * TAPS), BF16),
            pltpu.VMEM((256 * TAPS, 256), BF16),
            pltpu.VMEM((256 * TAPS, 256), BF16),
            pltpu.VMEM((8, 256, 256), BF16),
            pltpu.VMEM((256, 256), BF16),
            pltpu.VMEM((384, 256), F32),
            *[pltpu.VMEM((8, 8, 8, 128), BF16)] * 6,
            pltpu.VMEM((GROUPS, 2, NX, NZ, 16, 128), F32),
            *[pltpu.VMEM((GROUPS, 2, NX, NZ, 16, 128), BF16)] * 2,
            *[pltpu.VMEM((2, GROUPS, 2, NZ, 16, 128), BF16)] * 2,
            *[pltpu.VMEM((2, GROUPS, NZ, 16, 128), BF16)] * 2,
            *[pltpu.VMEM((NZ, GROUPS, 16, 256), BF16)] * 2,
            dma((2,)),
            dma((2, 2)),
            dma((2, 2)),
            dma((PARTS, 3, 2)),
            dma((PARTS, 3, 2)),
            dma((PARTS, NZ)),
            dma((PARTS, NZ)),
        ],
        compiler_params=pltpu.CompilerParams(
            collective_id=0, has_side_effects=True, vmem_limit_bytes=56 * 2**20
        ),
        cost_estimate=pl.CostEstimate(flops=7 * 10**9, bytes_accessed=6 * 10**6, transcendentals=0),
    )(
        features,
        conv_weight,
        down_weight,
        grad_conv,
        grad_down,
        live_rows,
        halo_send,
        neighbors,
        coarse_code.reshape(1, 256),
    )
    return pl.pallas_call(
        place,
        out_shape=tuple(jax.ShapeDtypeStruct(r.shape, r.dtype) for r in results),
        in_specs=[vmem] * 5,
        out_specs=[vmem] * 5,
    )(*results)


def solution(mesh):
    rows = P(("dp", "space"), None)
    return jax.shard_map(
        per_device,
        mesh=mesh,
        in_specs=(rows, P(), P(), rows, rows, P(("dp", "space")), rows, P(None, ("dp", "space")), P(("dp", "space"))),
        out_specs=(rows, rows, rows, P("dp", "space", None), P("dp", "space", None)),
        check_vma=False,
    )
```

```python
import jax
import jax.numpy as jnp
from jax import lax
from jax.experimental import pallas as pl
from jax.experimental.pallas import tpu as pltpu
from jax.sharding import PartitionSpec as P

MESH = pl.DeviceIdType.MESH
BF16, F32, I32 = jnp.bfloat16, jnp.float32, jnp.int32
NX, NZ = 4, 8
TAPS, GROUPS = 27, 9
CHUNKS = ((0, 1), (1, 3), (3, 5), (5, 7), (7, 9))
PARTS = len(CHUNKS)


def mm(a, b):
    return jnp.dot(a, b, preferred_element_type=F32)


def mm_nt(a, b):
    return lax.dot_general(a, b, (((1,), (1,)), ((), ())), preferred_element_type=F32)


def mm_tn(a, b):
    return lax.dot_general(a, b, (((0,), (0,)), ((), ())), preferred_element_type=F32)


def onehot(mask):
    return jnp.where(mask, 1.0, 0.0).astype(BF16)


def iota(shape, dim):
    return lax.broadcasted_iota(I32, shape, dim)


def tap(k):
    return slice(256 * k, 256 * k + 256)


def slot_row(q, kind, half, arriving):
    peer = q // 2
    line, column = (peer // 2) % NZ, 2 * (peer // 16) + peer % 2
    slot = 8 * column + line if arriving else 8 * line + column
    return 8 * slot + 2 * (2 * kind + q % 2) + half


def pack(first, second):
    row, q = iota((512, 128), 0), iota((512, 128), 1)
    total = jnp.zeros((512, 128), F32)
    for kind, rows in ((0, first), (1, second)):
        for half in range(2):
            place = onehot(row == slot_row(q, kind, half, False))
            total += mm(place, rows[:, half * 128 : half * 128 + 128])
    return total.reshape(8, 8, 8, 128).astype(BF16)


def unpack(slots, kind):
    q, row = iota((128, 512), 0), iota((128, 512), 1)
    flat = slots.astype(F32).reshape(512, 128).astype(BF16)
    return jnp.concatenate(
        [mm(onehot(row == slot_row(q, kind, half, True)), flat) for half in range(2)], axis=1
    )


def interleave(terms):
    a = [term.reshape(32, 8, 256) for term in terms]
    r = [pltpu.roll(value, 4, 1) for value in a]
    low = iota((32, 8, 256), 1) < 4
    first = jnp.concatenate(
        [jnp.where(low, a[0], r[1]), jnp.where(low, a[2], r[3])], axis=1
    )
    second = jnp.concatenate(
        [jnp.where(low, r[0], a[1]), jnp.where(low, r[2], a[3])], axis=1
    )
    return first, second


def kernel(
    feat_ref,
    w_hbm,
    wd_hbm,
    gconv_ref,
    gdown_ref,
    live_ref,
    send_ref,
    nbr_ref,
    code_ref,
    conv_ref,
    down_ref,
    gfeat_ref,
    wg_ref,
    dg_ref,
    w_ref,
    wd_ref,
    wt,
    oht,
    picked,
    pulled,
    cbo,
    total_ref,
    ext_grad,
    a1_src,
    a1_mid,
    a1_dst,
    a2_src,
    a2_mid,
    a2_dst,
    mine,
    give0,
    got0,
    give1,
    got1,
    give2,
    got2,
    give3,
    got3,
    w_sem,
    a_ss,
    a_rs,
    r_ss,
    r_rs,
    z_ss,
    z_rs,
):
    me = lax.axis_index("space")
    x, z, core = me // 16, (me // 2) % NZ, me % 2
    x1, x2, x3 = x + 1 - 2 * (x % 2), (x + 2) % NX, 3 - x

    column = 2 * x + core

    def device(xx, zz, cc):
        return {"space": (xx * NZ + zz) * 2 + cc}

    def in_line(i):
        return (z + i) % NZ

    def in_plane(i):
        return (column + i) % 8

    barrier = pltpu.get_barrier_semaphore()
    for i in range(1, 8):
        for to in (device(x, in_line(i), core), device(in_plane(i) // 2, z, in_plane(i) % 2)):
            pl.semaphore_signal(barrier, inc=1, device_id=to, device_id_type=MESH)
    w_copy = pltpu.make_async_copy(w_hbm, w_ref, w_sem.at[0])
    wd_copy = pltpu.make_async_copy(wd_hbm, wd_ref, w_sem.at[1])
    w_copy.start()
    wd_copy.start()

    def remote(src, dst, ss, rs, to):
        return pltpu.make_async_remote_copy(
            src_ref=src, dst_ref=dst, send_sem=ss, recv_sem=rs, device_id=to, device_id_type=MESH
        )

    def line_start(src, mid, which):
        ss, rs = a_ss.at[which, 0], a_rs.at[which, 0]
        for i in range(1, 8):
            to = in_line(i)
            remote(src.at[to], mid.at[z], ss, rs, device(x, to, core)).start()
        pltpu.make_async_copy(src.at[z], mid.at[z], rs).start()

    def line_wait(src, mid, which):
        pltpu.make_async_copy(src, mid, a_rs.at[which, 0]).wait()

    def plane_start(mid, dst, which):
        ss, rs = a_ss.at[which, 1], a_rs.at[which, 1]
        for i in range(1, 8):
            to = in_plane(i)
            remote(mid.at[:, to], dst.at[column], ss, rs, device(to // 2, z, to % 2)).start()
        pltpu.make_async_copy(mid.at[:, column], dst.at[column], rs).start()

    def plane_wait(mid, dst, which):
        pltpu.make_async_copy(mid, dst, a_rs.at[which, 1]).wait()

    def exchange_sent(buffer, which):
        rest = buffer.at[pl.ds(0, 7)]
        for phase in range(2):
            pltpu.make_async_copy(rest, rest, a_ss.at[which, phase]).wait()

    feat = feat_ref[...]
    send_hot = onehot(iota((256, 128), 0) == send_ref[...])
    a1_src[...] = pack(mm_tn(send_hot, feat).astype(BF16), gdown_ref[...])
    pl.semaphore_wait(barrier, 14)
    line_start(a1_src, a1_mid, 0)
    feat_t = feat.astype(F32).T.astype(BF16)
    source = iota((384, 256), 0)
    for k in range(TAPS):
        oht[:, tap(k)] = onehot(source == nbr_ref[k : k + 1, :])
    line_wait(a1_src, a1_mid, 0)
    plane_start(a1_mid, a1_dst, 0)
    for k in range(TAPS):
        picked[tap(k)] = mm(feat_t, oht[:256, tap(k)]).astype(BF16)
    w_copy.wait()
    for k in range(TAPS):
        wt[:, tap(k)] = w_ref[k].T
    wd_copy.wait()

    plane_wait(a1_mid, a1_dst, 0)
    arrived = a1_dst[...]
    halo_t = unpack(arrived, 0).T.astype(BF16)
    coarse_back = unpack(arrived, 1).astype(BF16)
    code_row = code_ref[...]
    code_col = jnp.broadcast_to(code_row.astype(F32), (8, 256)).T[:, :1].astype(I32)
    from_down = jnp.zeros((256, 256), F32)
    for o in range(8):
        rows = mm(onehot(code_col == 8 * iota((256, 128), 1) + o), coarse_back).astype(BF16)
        cbo[o] = rows
        from_down += mm_nt(rows, wd_ref[o])
    occupied = iota((256, 256), 0) < live_ref[0]
    total = jnp.where(occupied, gconv_ref[...].astype(F32) + from_down, 0.0).astype(BF16)
    total_ref[...] = total

    near, far = (x1, x3), (x3, x1)

    def span(c):
        return pl.ds(CHUNKS[c][0], CHUNKS[c][1] - CHUNKS[c][0])

    def copies(c, step):
        s = span(c)
        if step == 0:
            return [remote(give0.at[s], got0.at[s], r_ss.at[c, 0, 0], r_rs.at[c, 0, 0], device(x, z, 1 - core))]
        if step == 3:
            return [
                remote(give3.at[in_line(i), s], got3.at[z, s], z_ss.at[c, i], z_rs.at[c, i], device(x, in_line(i), core))
                for i in range(1, NZ)
            ]
        give, got, to = (give1, got1, near) if step == 1 else (give2, got2, far)
        return [
            remote(give.at[h, s], got.at[h, s], r_ss.at[c, step, h], r_rs.at[c, step, h], device(to[h], z, core))
            for h in range(2)
        ]

    def send(c, step):
        for copy in copies(c, step):
            copy.start()

    def receive(c, step):
        for copy in copies(c, step):
            copy.wait_recv()

    def give(g, terms):
        first, second = interleave(terms)
        own = jnp.where(core == 0, first, second)
        other = jnp.where(core == 0, second, first).astype(BF16)
        for h in range(2):
            half = slice(128 * h, 128 * h + 128)
            mine[g, h] = own[:, :, half].reshape(NX, NZ, 16, 128)
            give0[g, h] = other[:, :, half].reshape(NX, NZ, 16, 128)

    def step1(c):
        s = span(c)
        receive(c, 0)
        for h in range(2):
            for i, xx in enumerate((near[h], x2)):
                give1[h, s, i] = (mine[s, h, xx] + got0[s, h, xx].astype(F32)).astype(BF16)
        send(c, 1)
        for h in range(2):
            for xx in (x, far[h]):
                mine[s, h, xx] += got0[s, h, xx].astype(F32)

    def step2(c):
        s = span(c)
        receive(c, 1)
        for h in range(2):
            give2[h, s] = (mine[s, h, far[h]] + got1[h, s, 1].astype(F32)).astype(BF16)
        send(c, 2)
        for h in range(2):
            mine[s, h, x] += got1[h, s, 0].astype(F32)

    def step3(c):
        s = span(c)
        receive(c, 2)
        for h in range(2):
            value = mine[s, h, x] + got2[h, s].astype(F32)
            mine[s, h, x] = value
            for zz in range(NZ):
                give3[zz, s, :, 128 * h : 128 * h + 128] = value[:, zz].astype(BF16)
        send(c, 3)

    def final(c):
        receive(c, 3)
        for g in range(*CHUNKS[c]):
            value = jnp.concatenate([mine[g, h, x, z] for h in range(2)], axis=1)
            for i in range(1, NZ):
                value += got3[in_line(i), g].astype(F32)
            value = (value * (1.0 / 64.0)).reshape(4, 4, 256)
            if g < 6:
                wg_ref[4 * g : 4 * g + 4] = value
            elif g == 6:
                wg_ref[24:27] = value[:3]
            else:
                dg_ref[4 * g - 28 : 4 * g - 24] = value

    def conv_group(g):
        taps = range(4 * g, min(4 * g + 4, TAPS))
        for k in taps:
            picked[tap(k)] += mm(halo_t, oht[256:, tap(k)]).astype(BF16)
        terms = [mm(picked[tap(k)], total_ref[...]) for k in taps]
        give(g, terms + [jnp.zeros((256, 256), F32)] * (4 - len(terms)))

    def pull(lo, hi):
        for k in range(lo, hi):
            pulled[tap(k)] = mm(total_ref[...], wt[:, tap(k)]).astype(BF16)

    def scatter(lo, hi):
        span = slice(256 * lo, 256 * hi)
        return mm(oht[:, span], pulled[span])

    for c in range(4):
        for g in range(*CHUNKS[c]):
            conv_group(g)
        send(c, 0)
        if c > 0:
            step1(c - 1)
    summed_t = mm(wt[...], picked[...])
    step1(3)
    conv_out = jnp.where(occupied, summed_t.T, 0.0).astype(BF16)
    conv_ref[...] = conv_out
    conv_t = conv_out.T
    give(7, [mm(conv_t, cbo[o]) for o in range(4)])
    give(8, [mm(conv_t, cbo[o]) for o in range(4, 8)])
    send(4, 0)
    step2(0)
    coarse_part = jnp.zeros((128, 256), F32)
    for o in range(8):
        hot = onehot(code_row == 8 * iota((128, 256), 0) + o)
        coarse_part += mm(mm(hot, conv_out).astype(BF16), wd_ref[o])
    step1(4)
    pull(0, 27)
    step2(1)
    ext_grad[...] = scatter(0, 27)
    a2_src[...] = pack(coarse_part.astype(BF16), ext_grad[256:384].astype(BF16))
    line_start(a2_src, a2_mid, 1)
    step3(0)
    step2(2)
    step3(1)
    step2(3)
    step3(2)
    final(0)
    step2(4)
    line_wait(a2_src, a2_mid, 1)
    plane_start(a2_mid, a2_dst, 1)
    step3(3)
    final(1)
    step3(4)
    plane_wait(a2_mid, a2_dst, 1)
    arrived = a2_dst[...]
    down_ref[...] = unpack(arrived, 0).astype(BF16)
    returned = unpack(arrived, 1).astype(BF16)
    gfeat_ref[...] = (ext_grad[:256] + mm(send_hot, returned)).astype(BF16)
    final(2)
    final(3)
    final(4)
    exchange_sent(a1_src, 0)
    exchange_sent(a2_src, 1)
    for c in range(PARTS):
        for step in range(4):
            for copy in copies(c, step):
                copy.wait_send()


def place(*refs):
    for held, out in zip(refs[:5], refs[5:]):
        out[...] = held[...]


def per_device(features, conv_weight, down_weight, grad_conv, grad_down, live_rows, halo_send, neighbors, coarse_code):
    vmem = pl.BlockSpec(memory_space=pltpu.VMEM)
    hbm = pl.BlockSpec(memory_space=pl.ANY)
    dma = pltpu.SemaphoreType.DMA
    results = pl.pallas_call(
        kernel,
        out_shape=(
            jax.ShapeDtypeStruct((256, 256), BF16),
            jax.ShapeDtypeStruct((128, 256), BF16),
            jax.ShapeDtypeStruct((256, 256), BF16),
            jax.ShapeDtypeStruct((27, 4, 256), F32),
            jax.ShapeDtypeStruct((8, 4, 256), F32),
        ),
        in_specs=[vmem, hbm, hbm, vmem, vmem, pl.BlockSpec(memory_space=pltpu.SMEM), vmem, vmem, vmem],
        out_specs=[vmem] * 5,
        scratch_shapes=[
            pltpu.VMEM((27, 256, 256), BF16),
            pltpu.VMEM((8, 256, 256), BF16),
            pltpu.VMEM((256, 256 * TAPS), BF16),
            pltpu.VMEM((384, 256 * TAPS), BF16),
            pltpu.VMEM((256 * TAPS, 256), BF16),
            pltpu.VMEM((256 * TAPS, 256), BF16),
            pltpu.VMEM((8, 256, 256), BF16),
            pltpu.VMEM((256, 256), BF16),
            pltpu.VMEM((384, 256), F32),
            *[pltpu.VMEM((8, 8, 8, 128), BF16)] * 6,
            pltpu.VMEM((GROUPS, 2, NX, NZ, 16, 128), F32),
            *[pltpu.VMEM((GROUPS, 2, NX, NZ, 16, 128), BF16)] * 2,
            *[pltpu.VMEM((2, GROUPS, 2, NZ, 16, 128), BF16)] * 2,
            *[pltpu.VMEM((2, GROUPS, NZ, 16, 128), BF16)] * 2,
            *[pltpu.VMEM((NZ, GROUPS, 16, 256), BF16)] * 2,
            dma((2,)),
            dma((2, 2)),
            dma((2, 2)),
            dma((PARTS, 3, 2)),
            dma((PARTS, 3, 2)),
            dma((PARTS, NZ)),
            dma((PARTS, NZ)),
        ],
        compiler_params=pltpu.CompilerParams(
            collective_id=0, has_side_effects=True, vmem_limit_bytes=56 * 2**20
        ),
        cost_estimate=pl.CostEstimate(flops=7 * 10**9, bytes_accessed=6 * 10**6, transcendentals=0),
    )(
        features,
        conv_weight,
        down_weight,
        grad_conv,
        grad_down,
        live_rows,
        halo_send,
        neighbors,
        coarse_code.reshape(1, 256),
    )
    return pl.pallas_call(
        place,
        out_shape=tuple(jax.ShapeDtypeStruct(r.shape, r.dtype) for r in results),
        in_specs=[vmem] * 5,
        out_specs=[vmem] * 5,
    )(*results)


def solution(mesh):
    rows = P(("dp", "space"), None)
    return jax.shard_map(
        per_device,
        mesh=mesh,
        in_specs=(rows, P(), P(), rows, rows, P(("dp", "space")), rows, P(None, ("dp", "space")), P(("dp", "space"))),
        out_specs=(rows, rows, rows, P("dp", "space", None), P("dp", "space", None)),
        check_vma=False,
    )
```

```python
import jax
import jax.numpy as jnp
from jax import lax
from jax.experimental import pallas as pl
from jax.experimental.pallas import tpu as pltpu
from jax.sharding import PartitionSpec as P

MESH = pl.DeviceIdType.MESH
BF16, F32, I32 = jnp.bfloat16, jnp.float32, jnp.int32
NX, NZ = 4, 8
TAPS, GROUPS = 27, 9
CHUNKS = ((0, 1), (1, 3), (3, 5), (5, 7), (7, 9))
PARTS = len(CHUNKS)


def mm(a, b):
    return jnp.dot(a, b, preferred_element_type=F32)


def mm_nt(a, b):
    return lax.dot_general(a, b, (((1,), (1,)), ((), ())), preferred_element_type=F32)


def mm_tn(a, b):
    return lax.dot_general(a, b, (((0,), (0,)), ((), ())), preferred_element_type=F32)


def onehot(mask):
    return jnp.where(mask, 1.0, 0.0).astype(BF16)


def iota(shape, dim):
    return lax.broadcasted_iota(I32, shape, dim)


def tap(k):
    return slice(256 * k, 256 * k + 256)


def slot_row(q, kind, half, arriving):
    peer = q // 2
    line, column = (peer // 2) % NZ, 2 * (peer // 16) + peer % 2
    slot = 8 * column + line if arriving else 8 * line + column
    return 8 * slot + 2 * (2 * kind + q % 2) + half


def pack(first, second):
    row, q = iota((512, 128), 0), iota((512, 128), 1)
    total = jnp.zeros((512, 128), F32)
    for kind, rows in ((0, first), (1, second)):
        for half in range(2):
            place = onehot(row == slot_row(q, kind, half, False))
            total += mm(place, rows[:, half * 128 : half * 128 + 128])
    return total.reshape(8, 8, 8, 128).astype(BF16)


def unpack(slots, kind):
    q, row = iota((128, 512), 0), iota((128, 512), 1)
    flat = slots.astype(F32).reshape(512, 128).astype(BF16)
    return jnp.concatenate(
        [mm(onehot(row == slot_row(q, kind, half, True)), flat) for half in range(2)], axis=1
    )


def interleave(terms):
    a = [term.reshape(32, 8, 256) for term in terms]
    r = [pltpu.roll(value, 4, 1) for value in a]
    low = iota((32, 8, 256), 1) < 4
    first = jnp.concatenate(
        [jnp.where(low, a[0], r[1]), jnp.where(low, a[2], r[3])], axis=1
    )
    second = jnp.concatenate(
        [jnp.where(low, r[0], a[1]), jnp.where(low, r[2], a[3])], axis=1
    )
    return first, second


def kernel(
    feat_hbm,
    w_hbm,
    wd_hbm,
    gconv_hbm,
    gdown_hbm,
    live_ref,
    send_ref,
    nbr_hbm,
    code_ref,
    conv_hbm,
    down_hbm,
    gfeat_hbm,
    wg_ref,
    dg_ref,
    feat_ref,
    gconv_ref,
    gdown_ref,
    nbr_ref,
    conv_ref,
    down_ref,
    gfeat_ref,
    w_ref,
    wd_ref,
    wt,
    oht,
    picked,
    pulled,
    cbo,
    total_ref,
    ext_grad,
    a1_src,
    a1_mid,
    a1_dst,
    a2_src,
    a2_mid,
    a2_dst,
    mine,
    give0,
    got0,
    give1,
    got1,
    give2,
    got2,
    give3,
    got3,
    w_sem,
    io_sem,
    a_ss,
    a_rs,
    r_ss,
    r_rs,
    z_ss,
    z_rs,
):
    me = lax.axis_index("space")
    x, z, core = me // 16, (me // 2) % NZ, me % 2
    x1, x2, x3 = x + 1 - 2 * (x % 2), (x + 2) % NX, 3 - x

    column = 2 * x + core

    def device(xx, zz, cc):
        return {"space": (xx * NZ + zz) * 2 + cc}

    def in_line(i):
        return (z + i) % NZ

    def in_plane(i):
        return (column + i) % 8

    barrier = pltpu.get_barrier_semaphore()
    for i in range(1, 8):
        for to in (device(x, in_line(i), core), device(in_plane(i) // 2, z, in_plane(i) % 2)):
            pl.semaphore_signal(barrier, inc=1, device_id=to, device_id_type=MESH)
    loads = [
        pltpu.make_async_copy(held, ref, io_sem.at[i])
        for i, (held, ref) in enumerate(
            ((feat_hbm, feat_ref), (gdown_hbm, gdown_ref), (nbr_hbm, nbr_ref), (gconv_hbm, gconv_ref))
        )
    ]
    for load in loads:
        load.start()
    stores = [
        pltpu.make_async_copy(ref, held, io_sem.at[4 + i])
        for i, (ref, held) in enumerate(((conv_ref, conv_hbm), (down_ref, down_hbm), (gfeat_ref, gfeat_hbm)))
    ]
    w_copy = pltpu.make_async_copy(w_hbm, w_ref, w_sem.at[0])
    wd_copy = pltpu.make_async_copy(wd_hbm, wd_ref, w_sem.at[1])
    w_copy.start()
    wd_copy.start()

    def remote(src, dst, ss, rs, to):
        return pltpu.make_async_remote_copy(
            src_ref=src, dst_ref=dst, send_sem=ss, recv_sem=rs, device_id=to, device_id_type=MESH
        )

    def line_start(src, mid, which):
        ss, rs = a_ss.at[which, 0], a_rs.at[which, 0]
        for i in range(1, 8):
            to = in_line(i)
            remote(src.at[to], mid.at[z], ss, rs, device(x, to, core)).start()
        pltpu.make_async_copy(src.at[z], mid.at[z], rs).start()

    def line_wait(src, mid, which):
        pltpu.make_async_copy(src, mid, a_rs.at[which, 0]).wait()

    def plane_start(mid, dst, which):
        ss, rs = a_ss.at[which, 1], a_rs.at[which, 1]
        for i in range(1, 8):
            to = in_plane(i)
            remote(mid.at[:, to], dst.at[column], ss, rs, device(to // 2, z, to % 2)).start()
        pltpu.make_async_copy(mid.at[:, column], dst.at[column], rs).start()

    def plane_wait(mid, dst, which):
        pltpu.make_async_copy(mid, dst, a_rs.at[which, 1]).wait()

    def exchange_sent(buffer, which):
        rest = buffer.at[pl.ds(0, 7)]
        for phase in range(2):
            pltpu.make_async_copy(rest, rest, a_ss.at[which, phase]).wait()

    loads[0].wait()
    loads[1].wait()
    feat = feat_ref[...]
    send_hot = onehot(iota((256, 128), 0) == send_ref[...])
    a1_src[...] = pack(mm_tn(send_hot, feat).astype(BF16), gdown_ref[...])
    pl.semaphore_wait(barrier, 14)
    line_start(a1_src, a1_mid, 0)
    feat_t = feat.astype(F32).T.astype(BF16)
    source = iota((384, 256), 0)
    loads[2].wait()
    for k in range(TAPS):
        oht[:, tap(k)] = onehot(source == nbr_ref[k : k + 1, :])
    line_wait(a1_src, a1_mid, 0)
    plane_start(a1_mid, a1_dst, 0)
    for k in range(TAPS):
        picked[tap(k)] = mm(feat_t, oht[:256, tap(k)]).astype(BF16)
    w_copy.wait()
    for k in range(TAPS):
        wt[:, tap(k)] = w_ref[k].T
    wd_copy.wait()
    loads[3].wait()

    plane_wait(a1_mid, a1_dst, 0)
    arrived = a1_dst[...]
    halo_t = unpack(arrived, 0).T.astype(BF16)
    coarse_back = unpack(arrived, 1).astype(BF16)
    code_row = code_ref[...]
    code_col = jnp.broadcast_to(code_row.astype(F32), (8, 256)).T[:, :1].astype(I32)
    from_down = jnp.zeros((256, 256), F32)
    for o in range(8):
        rows = mm(onehot(code_col == 8 * iota((256, 128), 1) + o), coarse_back).astype(BF16)
        cbo[o] = rows
        from_down += mm_nt(rows, wd_ref[o])
    occupied = iota((256, 256), 0) < live_ref[0]
    total = jnp.where(occupied, gconv_ref[...].astype(F32) + from_down, 0.0).astype(BF16)
    total_ref[...] = total

    near, far = (x1, x3), (x3, x1)

    def span(c):
        return pl.ds(CHUNKS[c][0], CHUNKS[c][1] - CHUNKS[c][0])

    def copies(c, step):
        s = span(c)
        if step == 0:
            return [remote(give0.at[s], got0.at[s], r_ss.at[c, 0, 0], r_rs.at[c, 0, 0], device(x, z, 1 - core))]
        if step == 3:
            return [
                remote(give3.at[in_line(i), s], got3.at[z, s], z_ss.at[c, i], z_rs.at[c, i], device(x, in_line(i), core))
                for i in range(1, NZ)
            ]
        give, got, to = (give1, got1, near) if step == 1 else (give2, got2, far)
        return [
            remote(give.at[h, s], got.at[h, s], r_ss.at[c, step, h], r_rs.at[c, step, h], device(to[h], z, core))
            for h in range(2)
        ]

    def send(c, step):
        for copy in copies(c, step):
            copy.start()

    def receive(c, step):
        for copy in copies(c, step):
            copy.wait_recv()

    def give(g, terms):
        first, second = interleave(terms)
        own = jnp.where(core == 0, first, second)
        other = jnp.where(core == 0, second, first).astype(BF16)
        for h in range(2):
            half = slice(128 * h, 128 * h + 128)
            mine[g, h] = own[:, :, half].reshape(NX, NZ, 16, 128)
            give0[g, h] = other[:, :, half].reshape(NX, NZ, 16, 128)

    def step1(c):
        s = span(c)
        receive(c, 0)
        for h in range(2):
            for i, xx in enumerate((near[h], x2)):
                give1[h, s, i] = (mine[s, h, xx] + got0[s, h, xx].astype(F32)).astype(BF16)
        send(c, 1)
        for h in range(2):
            for xx in (x, far[h]):
                mine[s, h, xx] += got0[s, h, xx].astype(F32)

    def step2(c):
        s = span(c)
        receive(c, 1)
        for h in range(2):
            give2[h, s] = (mine[s, h, far[h]] + got1[h, s, 1].astype(F32)).astype(BF16)
        send(c, 2)
        for h in range(2):
            mine[s, h, x] += got1[h, s, 0].astype(F32)

    def step3(c):
        s = span(c)
        receive(c, 2)
        for h in range(2):
            value = mine[s, h, x] + got2[h, s].astype(F32)
            mine[s, h, x] = value
            for zz in range(NZ):
                give3[zz, s, :, 128 * h : 128 * h + 128] = value[:, zz].astype(BF16)
        send(c, 3)

    def final(c):
        receive(c, 3)
        for g in range(*CHUNKS[c]):
            value = jnp.concatenate([mine[g, h, x, z] for h in range(2)], axis=1)
            for i in range(1, NZ):
                value += got3[in_line(i), g].astype(F32)
            value = (value * (1.0 / 64.0)).reshape(4, 4, 256)
            if g < 6:
                wg_ref[4 * g : 4 * g + 4] = value
            elif g == 6:
                wg_ref[24:27] = value[:3]
            else:
                dg_ref[4 * g - 28 : 4 * g - 24] = value

    def conv_group(g):
        taps = range(4 * g, min(4 * g + 4, TAPS))
        for k in taps:
            picked[tap(k)] += mm(halo_t, oht[256:, tap(k)]).astype(BF16)
        terms = [mm(picked[tap(k)], total_ref[...]) for k in taps]
        give(g, terms + [jnp.zeros((256, 256), F32)] * (4 - len(terms)))

    def pull(lo, hi):
        for k in range(lo, hi):
            pulled[tap(k)] = mm(total_ref[...], wt[:, tap(k)]).astype(BF16)

    def scatter(lo, hi):
        span = slice(256 * lo, 256 * hi)
        return mm(oht[:, span], pulled[span])

    for c in range(4):
        for g in range(*CHUNKS[c]):
            conv_group(g)
        send(c, 0)
        if c > 0:
            step1(c - 1)
    summed_t = mm(wt[...], picked[...])
    step1(3)
    conv_out = jnp.where(occupied, summed_t.T, 0.0).astype(BF16)
    conv_ref[...] = conv_out
    stores[0].start()
    conv_t = conv_out.T
    give(7, [mm(conv_t, cbo[o]) for o in range(4)])
    give(8, [mm(conv_t, cbo[o]) for o in range(4, 8)])
    send(4, 0)
    step2(0)
    coarse_part = jnp.zeros((128, 256), F32)
    for o in range(8):
        hot = onehot(code_row == 8 * iota((128, 256), 0) + o)
        coarse_part += mm(mm(hot, conv_out).astype(BF16), wd_ref[o])
    step1(4)
    pull(0, 27)
    step2(1)
    ext_grad[...] = scatter(0, 27)
    a2_src[...] = pack(coarse_part.astype(BF16), ext_grad[256:384].astype(BF16))
    line_start(a2_src, a2_mid, 1)
    step3(0)
    step2(2)
    step3(1)
    step2(3)
    step3(2)
    final(0)
    step2(4)
    line_wait(a2_src, a2_mid, 1)
    plane_start(a2_mid, a2_dst, 1)
    step3(3)
    final(1)
    step3(4)
    plane_wait(a2_mid, a2_dst, 1)
    arrived = a2_dst[...]
    down_ref[...] = unpack(arrived, 0).astype(BF16)
    stores[1].start()
    returned = unpack(arrived, 1).astype(BF16)
    gfeat_ref[...] = (ext_grad[:256] + mm(send_hot, returned)).astype(BF16)
    stores[2].start()
    final(2)
    final(3)
    final(4)
    for store in stores:
        store.wait()
    exchange_sent(a1_src, 0)
    exchange_sent(a2_src, 1)
    for c in range(PARTS):
        for step in range(4):
            for copy in copies(c, step):
                copy.wait_send()


def place(*refs):
    for held, out in zip(refs[:5], refs[5:]):
        out[...] = held[...]


def per_device(features, conv_weight, down_weight, grad_conv, grad_down, live_rows, halo_send, neighbors, coarse_code):
    vmem = pl.BlockSpec(memory_space=pltpu.VMEM)
    hbm = pl.BlockSpec(memory_space=pl.ANY)
    dma = pltpu.SemaphoreType.DMA
    results = pl.pallas_call(
        kernel,
        out_shape=(
            jax.ShapeDtypeStruct((256, 256), BF16),
            jax.ShapeDtypeStruct((128, 256), BF16),
            jax.ShapeDtypeStruct((256, 256), BF16),
            jax.ShapeDtypeStruct((27, 4, 256), F32),
            jax.ShapeDtypeStruct((8, 4, 256), F32),
        ),
        in_specs=[hbm, hbm, hbm, hbm, hbm, pl.BlockSpec(memory_space=pltpu.SMEM), vmem, hbm, vmem],
        out_specs=[hbm, hbm, hbm, vmem, vmem],
        scratch_shapes=[
            pltpu.VMEM((256, 256), BF16),
            pltpu.VMEM((256, 256), BF16),
            pltpu.VMEM((128, 256), BF16),
            pltpu.VMEM((27, 256), I32),
            pltpu.VMEM((256, 256), BF16),
            pltpu.VMEM((128, 256), BF16),
            pltpu.VMEM((256, 256), BF16),
            pltpu.VMEM((27, 256, 256), BF16),
            pltpu.VMEM((8, 256, 256), BF16),
            pltpu.VMEM((256, 256 * TAPS), BF16),
            pltpu.VMEM((384, 256 * TAPS), BF16),
            pltpu.VMEM((256 * TAPS, 256), BF16),
            pltpu.VMEM((256 * TAPS, 256), BF16),
            pltpu.VMEM((8, 256, 256), BF16),
            pltpu.VMEM((256, 256), BF16),
            pltpu.VMEM((384, 256), F32),
            *[pltpu.VMEM((8, 8, 8, 128), BF16)] * 6,
            pltpu.VMEM((GROUPS, 2, NX, NZ, 16, 128), F32),
            *[pltpu.VMEM((GROUPS, 2, NX, NZ, 16, 128), BF16)] * 2,
            *[pltpu.VMEM((2, GROUPS, 2, NZ, 16, 128), BF16)] * 2,
            *[pltpu.VMEM((2, GROUPS, NZ, 16, 128), BF16)] * 2,
            *[pltpu.VMEM((NZ, GROUPS, 16, 256), BF16)] * 2,
            dma((2,)),
            dma((7,)),
            dma((2, 2)),
            dma((2, 2)),
            dma((PARTS, 3, 2)),
            dma((PARTS, 3, 2)),
            dma((PARTS, NZ)),
            dma((PARTS, NZ)),
        ],
        compiler_params=pltpu.CompilerParams(
            collective_id=0, has_side_effects=True, vmem_limit_bytes=56 * 2**20
        ),
        cost_estimate=pl.CostEstimate(flops=7 * 10**9, bytes_accessed=6 * 10**6, transcendentals=0),
    )(
        features,
        conv_weight,
        down_weight,
        grad_conv,
        grad_down,
        live_rows,
        halo_send,
        neighbors,
        coarse_code.reshape(1, 256),
    )
    return pl.pallas_call(
        place,
        out_shape=tuple(jax.ShapeDtypeStruct(r.shape, r.dtype) for r in results),
        in_specs=[vmem] * 5,
        out_specs=[vmem] * 5,
    )(*results)


def solution(mesh):
    rows = P(("dp", "space"), None)
    return jax.shard_map(
        per_device,
        mesh=mesh,
        in_specs=(rows, P(), P(), rows, rows, P(("dp", "space")), rows, P(None, ("dp", "space")), P(("dp", "space"))),
        out_specs=(rows, rows, rows, P("dp", "space", None), P("dp", "space", None)),
        check_vma=False,
    )
```

```python
import jax
import jax.numpy as jnp
from jax import lax
from jax.experimental import pallas as pl
from jax.experimental.pallas import tpu as pltpu
from jax.sharding import PartitionSpec as P

MESH = pl.DeviceIdType.MESH
BF16, F32, I32 = jnp.bfloat16, jnp.float32, jnp.int32
NX, NZ = 4, 8
TAPS, GROUPS = 27, 9
CHUNKS = ((0, 1), (1, 3), (3, 5), (5, 7), (7, 9))
PARTS = len(CHUNKS)


def mm(a, b):
    return jnp.dot(a, b, preferred_element_type=F32)


def mm_nt(a, b):
    return lax.dot_general(a, b, (((1,), (1,)), ((), ())), preferred_element_type=F32)


def mm_tn(a, b):
    return lax.dot_general(a, b, (((0,), (0,)), ((), ())), preferred_element_type=F32)


def onehot(mask):
    return jnp.where(mask, 1.0, 0.0).astype(BF16)


def iota(shape, dim):
    return lax.broadcasted_iota(I32, shape, dim)


def tap(k):
    return slice(256 * k, 256 * k + 256)


def slot_row(q, kind, half, arriving):
    peer = q // 2
    line, column = (peer // 2) % NZ, 2 * (peer // 16) + peer % 2
    slot = 8 * column + line if arriving else 8 * line + column
    return 8 * slot + 2 * (2 * kind + q % 2) + half


def pack(first, second):
    row, q = iota((512, 128), 0), iota((512, 128), 1)
    total = jnp.zeros((512, 128), F32)
    for kind, rows in ((0, first), (1, second)):
        for half in range(2):
            place = onehot(row == slot_row(q, kind, half, False))
            total += mm(place, rows[:, half * 128 : half * 128 + 128])
    return total.reshape(8, 8, 8, 128).astype(BF16)


def unpack(slots, kind):
    q, row = iota((128, 512), 0), iota((128, 512), 1)
    flat = slots.astype(F32).reshape(512, 128).astype(BF16)
    return jnp.concatenate(
        [mm(onehot(row == slot_row(q, kind, half, True)), flat) for half in range(2)], axis=1
    )


def interleave(terms):
    a = [term.reshape(32, 8, 256) for term in terms]
    r = [pltpu.roll(value, 4, 1) for value in a]
    low = iota((32, 8, 256), 1) < 4
    first = jnp.concatenate(
        [jnp.where(low, a[0], r[1]), jnp.where(low, a[2], r[3])], axis=1
    )
    second = jnp.concatenate(
        [jnp.where(low, r[0], a[1]), jnp.where(low, r[2], a[3])], axis=1
    )
    return first, second


def kernel(
    feat_hbm,
    w_hbm,
    wd_hbm,
    gconv_hbm,
    gdown_hbm,
    live_ref,
    send_ref,
    nbr_hbm,
    code_ref,
    conv_hbm,
    down_hbm,
    gfeat_hbm,
    wg_ref,
    dg_ref,
    feat_ref,
    gconv_ref,
    gdown_ref,
    nbr_ref,
    conv_ref,
    down_ref,
    gfeat_ref,
    w_ref,
    wd_ref,
    wt,
    oht,
    picked,
    pulled,
    cbo,
    total_ref,
    ext_grad,
    a1_src,
    a1_mid,
    a1_dst,
    a2_src,
    a2_mid,
    a2_dst,
    mine,
    give0,
    got0,
    give1,
    got1,
    give2,
    got2,
    give3,
    got3,
    w_sem,
    io_sem,
    a_ss,
    a_rs,
    r_ss,
    r_rs,
    z_ss,
    z_rs,
):
    me = lax.axis_index("space")
    x, z, core = me // 16, (me // 2) % NZ, me % 2
    x1, x2, x3 = x + 1 - 2 * (x % 2), (x + 2) % NX, 3 - x

    column = 2 * x + core

    def device(xx, zz, cc):
        return {"space": (xx * NZ + zz) * 2 + cc}

    def in_line(i):
        return (z + i) % NZ

    def in_plane(i):
        return (column + i) % 8

    barrier = pltpu.get_barrier_semaphore()
    for i in (4, 3, 5, 2, 6, 1, 7):
        for to in (device(x, in_line(i), core), device(in_plane(i) // 2, z, in_plane(i) % 2)):
            pl.semaphore_signal(barrier, inc=1, device_id=to, device_id_type=MESH)
    loads = [
        pltpu.make_async_copy(held, ref, io_sem.at[i])
        for i, (held, ref) in enumerate(
            ((feat_hbm, feat_ref), (gdown_hbm, gdown_ref), (nbr_hbm, nbr_ref), (gconv_hbm, gconv_ref))
        )
    ]
    for load in loads:
        load.start()
    stores = [
        pltpu.make_async_copy(ref, held, io_sem.at[4 + i])
        for i, (ref, held) in enumerate(((conv_ref, conv_hbm), (down_ref, down_hbm), (gfeat_ref, gfeat_hbm)))
    ]
    w_copy = pltpu.make_async_copy(w_hbm, w_ref, w_sem.at[0])
    wd_copy = pltpu.make_async_copy(wd_hbm, wd_ref, w_sem.at[1])
    w_copy.start()
    wd_copy.start()

    def remote(src, dst, ss, rs, to):
        return pltpu.make_async_remote_copy(
            src_ref=src, dst_ref=dst, send_sem=ss, recv_sem=rs, device_id=to, device_id_type=MESH
        )

    def line_start(src, mid, which):
        ss, rs = a_ss.at[which, 0], a_rs.at[which, 0]
        for i in (4, 3, 5, 2, 6, 1, 7):
            to = in_line(i)
            remote(src.at[to], mid.at[z], ss, rs, device(x, to, core)).start()
        pltpu.make_async_copy(src.at[z], mid.at[z], rs).start()

    def line_wait(src, mid, which):
        pltpu.make_async_copy(src, mid, a_rs.at[which, 0]).wait()

    def plane_start(mid, dst, which):
        ss, rs = a_ss.at[which, 1], a_rs.at[which, 1]
        for i in (4, 3, 5, 2, 6, 1, 7):
            to = in_plane(i)
            remote(mid.at[:, to], dst.at[column], ss, rs, device(to // 2, z, to % 2)).start()
        pltpu.make_async_copy(mid.at[:, column], dst.at[column], rs).start()

    def plane_wait(mid, dst, which):
        pltpu.make_async_copy(mid, dst, a_rs.at[which, 1]).wait()

    def exchange_sent(buffer, which):
        rest = buffer.at[pl.ds(0, 7)]
        for phase in range(2):
            pltpu.make_async_copy(rest, rest, a_ss.at[which, phase]).wait()

    loads[0].wait()
    loads[1].wait()
    feat = feat_ref[...]
    send_hot = onehot(iota((256, 128), 0) == send_ref[...])
    a1_src[...] = pack(mm_tn(send_hot, feat).astype(BF16), gdown_ref[...])
    pl.semaphore_wait(barrier, 14)
    line_start(a1_src, a1_mid, 0)
    feat_t = feat.astype(F32).T.astype(BF16)
    source = iota((384, 256), 0)
    loads[2].wait()
    for k in range(TAPS):
        oht[:, tap(k)] = onehot(source == nbr_ref[k : k + 1, :])
    line_wait(a1_src, a1_mid, 0)
    plane_start(a1_mid, a1_dst, 0)
    for k in range(TAPS):
        picked[tap(k)] = mm(feat_t, oht[:256, tap(k)]).astype(BF16)
    w_copy.wait()
    for k in range(TAPS):
        wt[:, tap(k)] = w_ref[k].T
    wd_copy.wait()
    loads[3].wait()

    plane_wait(a1_mid, a1_dst, 0)
    arrived = a1_dst[...]
    halo_t = unpack(arrived, 0).T.astype(BF16)
    coarse_back = unpack(arrived, 1).astype(BF16)
    code_row = code_ref[...]
    code_col = jnp.broadcast_to(code_row.astype(F32), (8, 256)).T[:, :1].astype(I32)
    from_down = jnp.zeros((256, 256), F32)
    for o in range(8):
        rows = mm(onehot(code_col == 8 * iota((256, 128), 1) + o), coarse_back).astype(BF16)
        cbo[o] = rows
        from_down += mm_nt(rows, wd_ref[o])
    occupied = iota((256, 256), 0) < live_ref[0]
    total = jnp.where(occupied, gconv_ref[...].astype(F32) + from_down, 0.0).astype(BF16)
    total_ref[...] = total

    near, far = (x1, x3), (x3, x1)

    def span(c):
        return pl.ds(CHUNKS[c][0], CHUNKS[c][1] - CHUNKS[c][0])

    def copies(c, step):
        s = span(c)
        if step == 0:
            return [remote(give0.at[s], got0.at[s], r_ss.at[c, 0, 0], r_rs.at[c, 0, 0], device(x, z, 1 - core))]
        if step == 3:
            return [
                remote(give3.at[in_line(i), s], got3.at[z, s], z_ss.at[c, i], z_rs.at[c, i], device(x, in_line(i), core))
                for i in range(1, NZ)
            ]
        give, got, to = (give1, got1, near) if step == 1 else (give2, got2, far)
        return [
            remote(give.at[h, s], got.at[h, s], r_ss.at[c, step, h], r_rs.at[c, step, h], device(to[h], z, core))
            for h in range(2)
        ]

    def send(c, step):
        for copy in copies(c, step):
            copy.start()

    def receive(c, step):
        for copy in copies(c, step):
            copy.wait_recv()

    def give(g, terms):
        first, second = interleave(terms)
        own = jnp.where(core == 0, first, second)
        other = jnp.where(core == 0, second, first).astype(BF16)
        for h in range(2):
            half = slice(128 * h, 128 * h + 128)
            mine[g, h] = own[:, :, half].reshape(NX, NZ, 16, 128)
            give0[g, h] = other[:, :, half].reshape(NX, NZ, 16, 128)

    def step1(c):
        s = span(c)
        receive(c, 0)
        for h in range(2):
            for i, xx in enumerate((near[h], x2)):
                give1[h, s, i] = (mine[s, h, xx] + got0[s, h, xx].astype(F32)).astype(BF16)
        send(c, 1)
        for h in range(2):
            for xx in (x, far[h]):
                mine[s, h, xx] += got0[s, h, xx].astype(F32)

    def step2(c):
        s = span(c)
        receive(c, 1)
        for h in range(2):
            give2[h, s] = (mine[s, h, far[h]] + got1[h, s, 1].astype(F32)).astype(BF16)
        send(c, 2)
        for h in range(2):
            mine[s, h, x] += got1[h, s, 0].astype(F32)

    def step3(c):
        s = span(c)
        receive(c, 2)
        for h in range(2):
            value = mine[s, h, x] + got2[h, s].astype(F32)
            mine[s, h, x] = value
            for zz in range(NZ):
                give3[zz, s, :, 128 * h : 128 * h + 128] = value[:, zz].astype(BF16)
        send(c, 3)

    def final(c):
        receive(c, 3)
        for g in range(*CHUNKS[c]):
            value = jnp.concatenate([mine[g, h, x, z] for h in range(2)], axis=1)
            for i in range(1, NZ):
                value += got3[in_line(i), g].astype(F32)
            value = (value * (1.0 / 64.0)).reshape(4, 4, 256)
            if g < 6:
                wg_ref[4 * g : 4 * g + 4] = value
            elif g == 6:
                wg_ref[24:27] = value[:3]
            else:
                dg_ref[4 * g - 28 : 4 * g - 24] = value

    def conv_group(g):
        taps = range(4 * g, min(4 * g + 4, TAPS))
        for k in taps:
            picked[tap(k)] += mm(halo_t, oht[256:, tap(k)]).astype(BF16)
        terms = [mm(picked[tap(k)], total_ref[...]) for k in taps]
        give(g, terms + [jnp.zeros((256, 256), F32)] * (4 - len(terms)))

    def pull(lo, hi):
        for k in range(lo, hi):
            pulled[tap(k)] = mm(total_ref[...], wt[:, tap(k)]).astype(BF16)

    def scatter(lo, hi):
        span = slice(256 * lo, 256 * hi)
        return mm(oht[:, span], pulled[span])

    for c in range(4):
        for g in range(*CHUNKS[c]):
            conv_group(g)
        send(c, 0)
        if c > 0:
            step1(c - 1)
    summed_t = mm(wt[...], picked[...])
    step1(3)
    conv_out = jnp.where(occupied, summed_t.T, 0.0).astype(BF16)
    conv_ref[...] = conv_out
    stores[0].start()
    conv_t = conv_out.T
    give(7, [mm(conv_t, cbo[o]) for o in range(4)])
    give(8, [mm(conv_t, cbo[o]) for o in range(4, 8)])
    send(4, 0)
    step2(0)
    coarse_part = jnp.zeros((128, 256), F32)
    for o in range(8):
        hot = onehot(code_row == 8 * iota((128, 256), 0) + o)
        coarse_part += mm(mm(hot, conv_out).astype(BF16), wd_ref[o])
    step1(4)
    pull(0, 27)
    step2(1)
    ext_grad[...] = scatter(0, 27)
    a2_src[...] = pack(coarse_part.astype(BF16), ext_grad[256:384].astype(BF16))
    line_start(a2_src, a2_mid, 1)
    step3(0)
    step2(2)
    step3(1)
    step2(3)
    step3(2)
    final(0)
    step2(4)
    line_wait(a2_src, a2_mid, 1)
    plane_start(a2_mid, a2_dst, 1)
    step3(3)
    final(1)
    step3(4)
    plane_wait(a2_mid, a2_dst, 1)
    arrived = a2_dst[...]
    down_ref[...] = unpack(arrived, 0).astype(BF16)
    stores[1].start()
    returned = unpack(arrived, 1).astype(BF16)
    gfeat_ref[...] = (ext_grad[:256] + mm(send_hot, returned)).astype(BF16)
    stores[2].start()
    final(2)
    final(3)
    final(4)
    for store in stores:
        store.wait()
    exchange_sent(a1_src, 0)
    exchange_sent(a2_src, 1)
    for c in range(PARTS):
        for step in range(4):
            for copy in copies(c, step):
                copy.wait_send()


def place(*refs):
    for held, out in zip(refs[:5], refs[5:]):
        out[...] = held[...]


def per_device(features, conv_weight, down_weight, grad_conv, grad_down, live_rows, halo_send, neighbors, coarse_code):
    vmem = pl.BlockSpec(memory_space=pltpu.VMEM)
    hbm = pl.BlockSpec(memory_space=pl.ANY)
    dma = pltpu.SemaphoreType.DMA
    results = pl.pallas_call(
        kernel,
        out_shape=(
            jax.ShapeDtypeStruct((256, 256), BF16),
            jax.ShapeDtypeStruct((128, 256), BF16),
            jax.ShapeDtypeStruct((256, 256), BF16),
            jax.ShapeDtypeStruct((27, 4, 256), F32),
            jax.ShapeDtypeStruct((8, 4, 256), F32),
        ),
        in_specs=[hbm, hbm, hbm, hbm, hbm, pl.BlockSpec(memory_space=pltpu.SMEM), vmem, hbm, vmem],
        out_specs=[hbm, hbm, hbm, vmem, vmem],
        scratch_shapes=[
            pltpu.VMEM((256, 256), BF16),
            pltpu.VMEM((256, 256), BF16),
            pltpu.VMEM((128, 256), BF16),
            pltpu.VMEM((27, 256), I32),
            pltpu.VMEM((256, 256), BF16),
            pltpu.VMEM((128, 256), BF16),
            pltpu.VMEM((256, 256), BF16),
            pltpu.VMEM((27, 256, 256), BF16),
            pltpu.VMEM((8, 256, 256), BF16),
            pltpu.VMEM((256, 256 * TAPS), BF16),
            pltpu.VMEM((384, 256 * TAPS), BF16),
            pltpu.VMEM((256 * TAPS, 256), BF16),
            pltpu.VMEM((256 * TAPS, 256), BF16),
            pltpu.VMEM((8, 256, 256), BF16),
            pltpu.VMEM((256, 256), BF16),
            pltpu.VMEM((384, 256), F32),
            *[pltpu.VMEM((8, 8, 8, 128), BF16)] * 6,
            pltpu.VMEM((GROUPS, 2, NX, NZ, 16, 128), F32),
            *[pltpu.VMEM((GROUPS, 2, NX, NZ, 16, 128), BF16)] * 2,
            *[pltpu.VMEM((2, GROUPS, 2, NZ, 16, 128), BF16)] * 2,
            *[pltpu.VMEM((2, GROUPS, NZ, 16, 128), BF16)] * 2,
            *[pltpu.VMEM((NZ, GROUPS, 16, 256), BF16)] * 2,
            dma((2,)),
            dma((7,)),
            dma((2, 2)),
            dma((2, 2)),
            dma((PARTS, 3, 2)),
            dma((PARTS, 3, 2)),
            dma((PARTS, NZ)),
            dma((PARTS, NZ)),
        ],
        compiler_params=pltpu.CompilerParams(
            collective_id=0, has_side_effects=True, vmem_limit_bytes=56 * 2**20
        ),
        cost_estimate=pl.CostEstimate(flops=7 * 10**9, bytes_accessed=6 * 10**6, transcendentals=0),
    )(
        features,
        conv_weight,
        down_weight,
        grad_conv,
        grad_down,
        live_rows,
        halo_send,
        neighbors,
        coarse_code.reshape(1, 256),
    )
    return pl.pallas_call(
        place,
        out_shape=tuple(jax.ShapeDtypeStruct(r.shape, r.dtype) for r in results),
        in_specs=[vmem] * 5,
        out_specs=[vmem] * 5,
    )(*results)


def solution(mesh):
    rows = P(("dp", "space"), None)
    return jax.shard_map(
        per_device,
        mesh=mesh,
        in_specs=(rows, P(), P(), rows, rows, P(("dp", "space")), rows, P(None, ("dp", "space")), P(("dp", "space"))),
        out_specs=(rows, rows, rows, P("dp", "space", None), P("dp", "space", None)),
        check_vma=False,
    )
```
